256 devices in a mesh: dom: 16 (over y, x), edge: 16 (over z, core).
Axes of the slice: x: 4, y: 4, z: 8, core: 2. Of those that a mesh axis runs over, the one named last changes fastest.
Arguments:
- src_table: float32 [400, 131072], P(None, ('dom', 'edge')), may hold values from -2.5 to 2.5
- src_state: float32 [131072], P(('dom', 'edge')), may hold values from 0.001 to 1
- dst_table: float32 [400, 131072], P(None, ('dom', 'edge')), may hold values from -2.5 to 2.5
- dst_state: float32 [131072], P(('dom', 'edge')), may hold values from 0.001 to 1
- relation: float32 [400, 16], replicated, may hold values from -4 to 4
- edge_src: int32 [1048576], P(('dom', 'edge')), may hold values from 0 to 511
- edge_dst: int32 [1048576], P(('dom', 'edge')), may hold values from 0 to 511
- edge_rel: int32 [1048576], P(('dom', 'edge')), may hold values from 0 to 15
- matching: int32 [16], replicated, may hold values from 0 to 15, as said below
- neg_rows: int32 [256, 16, 256], P(('dom', 'edge')), may hold values from 0 to 511
- quotas: int32 [256, 16], P(('dom', 'edge')), may hold values from 0 to 2, as said below
Outputs:
- src_out: float32 [400, 131072], P(None, ('dom', 'edge'))
- src_state_out: float32 [131072], P(('dom', 'edge'))
- dst_out: float32 [400, 131072], P(None, ('dom', 'edge'))
- dst_state_out: float32 [131072], P(('dom', 'edge'))
- relation_out: float32 [400, 16], replicated
The draws below stay inside these ranges and needn't reach their ends.
Inputs may be any that keep to these rules, and one draw needn't show every extreme that they name: matching names every partition exactly once. `quotas`: each device's 16 entries sum to exactly 12; for each index of dom, one index of edge is given 2 blocks by every device of that index of dom.
All inputs are finite; a program needn't handle non-finite values.
Results may differ from the reference program's by a relative error of at most 0.0011.
Values may be sent and summed in bfloat16 or wider, within the bound.
A program may use at most 128 MiB of HBM per device.

```python
import math
import jax
import jax.numpy as jnp
import numpy as np
from jax import lax

DIM = 400
NREL = 16
ROWS_DEV = 512
E_DEV = 4096
BLOCK = 128
QMAX = 2
QTOTAL = 12
NNEG = 1536
SLOTS = 256
ROWS_ALL = 131072
EDGES_ALL = 1048576
N_DOM = 16
N_EDGE = 16


def draw_matching(key, part):
    base_key = jax.random.fold_in(key, 11)
    shuffled = jax.random.permutation(jax.random.fold_in(base_key, 1), N_DOM).astype(jnp.int32)
    chosen = jax.random.randint(jax.random.fold_in(base_key, 2), (), 0, N_DOM, dtype=jnp.int32)
    target = ((chosen + N_DOM // 2) % N_DOM).astype(jnp.int32)
    places = jnp.arange(N_DOM, dtype=jnp.int32)
    where_target = jnp.sum(jnp.where(shuffled == target, places, 0)).astype(jnp.int32)
    held_value = jnp.sum(jnp.where(places == chosen, shuffled, 0)).astype(jnp.int32)
    result = jnp.where(places == chosen, target, jnp.where(places == where_target, held_value, shuffled))
    return result.astype(jnp.int32)


def draw_quotas(key, part):
    base_key = jax.random.fold_in(key, 23)
    heavy = jax.random.randint(jax.random.fold_in(base_key, 1), (N_DOM,), 0, N_EDGE, dtype=jnp.int32)
    row_keys = jax.random.split(jax.random.fold_in(base_key, 2), N_DOM * N_EDGE)
    shard_ids = jnp.arange(N_EDGE, dtype=jnp.int32)

    def one_device(row_key, dom_heavy):
        shuffled = jax.random.permutation(row_key, QMAX * (N_EDGE - 1)).astype(jnp.int32)
        chosen = shuffled[:QTOTAL - QMAX] // QMAX
        target = chosen + (chosen >= dom_heavy).astype(jnp.int32)
        counts = jnp.sum((target[:, None] == shard_ids[None, :]).astype(jnp.int32), axis=0)
        return (counts + QMAX * (shard_ids == dom_heavy).astype(jnp.int32)).astype(jnp.int32)
    return jax.vmap(one_device)(row_keys, jnp.repeat(heavy, N_EDGE)).astype(jnp.int32)


def plant(array, own_key, least, high):
    extent = array.shape
    place = [jax.random.randint(jax.random.fold_in(own_key, axis), (), 0, extent[axis]) for axis in range(len(extent))]
    array = array.at[tuple(place)].set(least)
    longest = extent.index(max(extent))
    place[longest] = (place[longest] + 1) % extent[longest]
    return array.at[tuple(place)].set(high)


def level_of(rng, shape, shards, low, largest):
    gain = 1.0
    for axis_at, shards_of in shards:
        steps = jax.random.uniform(jax.random.fold_in(jax.random.fold_in(rng, 6), axis_at), (shards_of,), jnp.float32, low / len(shards), largest / len(shards))
        gain = gain * jnp.repeat(jnp.exp(steps), shape[axis_at] // shards_of).reshape((-1,) + (1,) * (len(shape) - 1 - axis_at))
    return gain


def rank_bounds(amount, slope):
    weights = [(1 << 20) // math.isqrt(grade ** slope) + 1 for grade in range(1, amount + 1)]
    scale = 1 + sum(weights) // (1 << 30)
    return np.cumsum(np.array([max(1, weight // scale) for weight in weights]))


def ranked_ids(key, dims, amount, skew):
    listing = rank_bounds(amount, skew)
    ticket = jax.random.randint(jax.random.fold_in(key, 1), dims, 0, int(listing[amount - 1]))
    rank = jnp.searchsorted(jnp.asarray(listing, jnp.int32), ticket, side="right")
    return jax.random.permutation(jax.random.fold_in(key, 2), amount)[rank].astype(jnp.int32)


def normal_values(stream_key, shape, scale, limit, cuts=(), kind=jnp.bfloat16):
    loudness = level_of(stream_key, shape, cuts, -0.22, 0.18) if cuts else 1.0
    drawn = jax.random.normal(stream_key, shape, jnp.float32) * scale * loudness
    return jnp.minimum(jnp.maximum(drawn, -limit), limit).astype(kind)


def setup_inputs(seed: int = 0) -> dict:
    arg_keys = jax.random.split(jax.random.key(seed), 12)
    src_table = normal_values(arg_keys[0], (DIM, ROWS_ALL), 0.4, 2.5, ((1, 256),), jnp.float32)
    src_state = jnp.clip(jnp.exp(math.log(1.0) - 6.9077552 * jax.random.uniform(arg_keys[1], (ROWS_ALL,), jnp.float32) ** level_of(arg_keys[1], (ROWS_ALL,), ((0, 256),), -0.2, 0.2)), 0.001, 1.0)
    dst_table = normal_values(arg_keys[2], (DIM, ROWS_ALL), 0.4, 2.5, ((1, 256),), jnp.float32)
    dst_state = jnp.clip(jnp.exp(math.log(1.0) - 6.9077552 * jax.random.uniform(arg_keys[3], (ROWS_ALL,), jnp.float32) ** level_of(arg_keys[3], (ROWS_ALL,), ((0, 256),), -0.2, 0.2)), 0.001, 1.0)
    relation = normal_values(arg_keys[4], (DIM, NREL), 0.7, 4.0, (), jnp.float32)
    edge_src = plant(jax.random.randint(arg_keys[5], (EDGES_ALL,), 0, ROWS_DEV), jax.random.fold_in(arg_keys[5], 1), 0, ROWS_DEV - 1).astype(jnp.int32)
    edge_dst = plant(ranked_ids(arg_keys[6], (EDGES_ALL,), ROWS_DEV, 2), jax.random.fold_in(arg_keys[6], 3), 0, ROWS_DEV - 1).astype(jnp.int32)
    edge_rel = plant(ranked_ids(arg_keys[7], (EDGES_ALL,), NREL, 1), jax.random.fold_in(arg_keys[7], 3), 0, NREL - 1).astype(jnp.int32)
    matching = draw_matching(jax.random.fold_in(arg_keys[11], 71), 0)
    neg_rows = plant(ranked_ids(arg_keys[9], (N_DOM * N_EDGE, N_EDGE, SLOTS), ROWS_DEV, 2), jax.random.fold_in(arg_keys[9], 3), 0, ROWS_DEV - 1).astype(jnp.int32)
    quotas = draw_quotas(jax.random.fold_in(arg_keys[11], 71), 0)
    return dict(src_table=src_table, src_state=src_state, dst_table=dst_table, dst_state=dst_state, relation=relation, edge_src=edge_src, edge_dst=edge_dst, edge_rel=edge_rel, matching=matching, neg_rows=neg_rows, quotas=quotas)


learn_rate = 0.1
rel_rate = 0.02

def complex_product(one_side, other_side):
    half_dim = one_side.shape[0] // 2
    real_part = one_side[:half_dim] * other_side[:half_dim] - one_side[half_dim:] * other_side[half_dim:]
    imag_part = one_side[:half_dim] * other_side[half_dim:] + one_side[half_dim:] * other_side[:half_dim]
    return jnp.concatenate([real_part, imag_part], axis=0)

def conj_product(gradient, operand):
    half_dim = gradient.shape[0] // 2
    real_part = gradient[:half_dim] * operand[:half_dim] + gradient[half_dim:] * operand[half_dim:]
    imag_part = gradient[half_dim:] * operand[:half_dim] - gradient[:half_dim] * operand[half_dim:]
    return jnp.concatenate([real_part, imag_part], axis=0)

def block_plan(quota_row, edge_count):
    block_ends = jnp.cumsum(quota_row).astype(jnp.int32)
    starts = (block_ends - quota_row).astype(jnp.int32)
    positions = jnp.arange(QTOTAL, dtype=jnp.int32)
    owner_of = lax.optimization_barrier(jnp.sum((block_ends[None, :] <= positions[:, None]).astype(jnp.int32), axis=1)).astype(jnp.int32)
    matches = owner_of[:, None] == jnp.arange(edge_count, dtype=jnp.int32)[None, :]
    first_block = lax.optimization_barrier(jnp.sum(jnp.where(matches, starts[None, :], 0), axis=1)).astype(jnp.int32)
    return (owner_of, (owner_of * QMAX + positions - first_block).astype(jnp.int32))

def adagrad(table_in, state_in, gradient):
    new_state = state_in + lax.optimization_barrier(jnp.mean(gradient * gradient, axis=-2))
    return (table_in - learn_rate * gradient / jnp.sqrt(new_state)[..., None, :], new_state)

def reference(src_table, src_state, dst_table, dst_state, relation, edge_src, edge_dst, edge_rel, matching, neg_rows, quotas):

    def as_blocks(table_in):
        return jnp.transpose(table_in.reshape(DIM, N_DOM, N_EDGE, ROWS_DEV), (1, 2, 0, 3))
    src_blocks = as_blocks(src_table)
    dst_blocks = as_blocks(dst_table)[matching]
    src_states = src_state.reshape(N_DOM, N_EDGE, ROWS_DEV)
    dst_states = dst_state.reshape(N_DOM, N_EDGE, ROWS_DEV)[matching]
    src_all = edge_src.reshape(N_DOM, N_EDGE, E_DEV)
    dst_all = edge_dst.reshape(N_DOM, N_EDGE, E_DEV)
    rel_all = edge_rel.reshape(N_DOM, N_EDGE, E_DEV)
    neg_all = neg_rows.reshape(N_DOM, N_EDGE, N_EDGE * QMAX, BLOCK)
    quota_all = quotas.reshape(N_DOM, N_EDGE, N_EDGE)
    weight = 1.0 / math.sqrt(NNEG)
    labels = jnp.arange(NREL, dtype=jnp.int32)

    def dom_row(inputs):
        src_tabs, part_tabs, src_sts, part_sts, src_ids, dst_ids, rel_ids, neg_ids, quota_rows = inputs

        def requester(totals, item_set):
            dst_grad, rel_grad = totals
            own_shard, src_tab, src_e, dst_e, rel_e, neg_e, quota_e = item_set
            onehot = (rel_e[None, :] == labels[:, None]).astype(jnp.float32)
            rel_edges = jnp.dot(relation, onehot, precision=lax.Precision.HIGHEST)
            src_rows = src_tab[:, src_e]
            dst_rows = part_tabs[own_shard][:, dst_e]
            queries = complex_product(src_rows, rel_edges)
            positive = lax.optimization_barrier(jnp.sum(queries * dst_rows, axis=0))
            pos_coef = -jax.nn.sigmoid(-positive)
            owner_of, block_at = block_plan(quota_e, N_EDGE)
            row_ids = neg_e[block_at]
            picked = part_tabs[owner_of[:, None], :, row_ids].astype(jnp.bfloat16)
            negatives = jnp.transpose(picked, (2, 0, 1)).reshape(DIM, NNEG)
            query_b = queries.astype(jnp.bfloat16)
            scores = jnp.dot(query_b.T, negatives, preferred_element_type=jnp.float32)
            neg_coef = (weight * jax.nn.sigmoid(scores)).astype(jnp.bfloat16)
            neg_grad = jnp.dot(query_b, neg_coef, preferred_element_type=jnp.float32)
            query_grad = pos_coef[None, :] * dst_rows + jnp.dot(negatives, neg_coef.T, preferred_element_type=jnp.float32)
            src_grad = jnp.zeros((DIM, ROWS_DEV), jnp.float32).at[:, src_e].add(conj_product(query_grad, rel_edges))
            own_grad = jnp.zeros((DIM, ROWS_DEV), jnp.float32).at[:, dst_e].add(pos_coef[None, :] * queries)
            dst_grad = dst_grad.at[own_shard].add(own_grad)
            spread = jnp.transpose(neg_grad.reshape(DIM, QTOTAL, BLOCK), (1, 2, 0))
            dst_grad = dst_grad.at[owner_of[:, None], :, row_ids].add(spread)
            rel_grad = rel_grad + jnp.dot(conj_product(query_grad, src_rows), onehot.T, precision=lax.Precision.HIGHEST)
            return ((dst_grad, rel_grad), src_grad)
        shard_ids = jnp.arange(N_EDGE, dtype=jnp.int32)
        start_totals = (jnp.zeros((N_EDGE, DIM, ROWS_DEV), jnp.float32), jnp.zeros((DIM, NREL), jnp.float32))
        summed, src_grads = lax.scan(requester, start_totals, (shard_ids, src_tabs, src_ids, dst_ids, rel_ids, neg_ids, quota_rows))
        dst_grads, rel_grad = summed
        src_new, src_st_new = adagrad(src_tabs, src_sts, src_grads)
        dst_new, dst_st_new = adagrad(part_tabs, part_sts, dst_grads)
        return (src_new, src_st_new, dst_new, dst_st_new, rel_grad)
    src_new, src_st_new, dst_new, dst_st_new, rel_grads = lax.map(dom_row, (src_blocks, dst_blocks, src_states, dst_states, src_all, dst_all, rel_all, neg_all, quota_all))
    relation_grad = lax.optimization_barrier(jnp.sum(rel_grads, axis=0))
    src_out = jnp.transpose(src_new, (2, 0, 1, 3)).reshape(DIM, ROWS_ALL)
    dst_out = jnp.transpose(dst_new, (2, 0, 1, 3)).reshape(DIM, ROWS_ALL)
    relation_out = relation - rel_rate * relation_grad
    return (src_out, src_st_new.reshape(ROWS_ALL), dst_out, dst_st_new.reshape(ROWS_ALL), relation_out)
```

```python
import math

import jax
import jax.numpy as jnp
from jax import lax
from jax.experimental import pallas as pl
from jax.experimental.pallas import tpu as pltpu
from jax.sharding import PartitionSpec as P

DIM = 400
HALF = 200
NREL = 16
BLOCK = 128
QMAX = 2
QTOTAL = 12
NNEG = 1536
ROWS = 512
EDGES = 4096
N_DOM = 16
N_EDGE = 16
N_Z = 8
FAR = N_Z // 2

PIECE_ROWS = 112
PIECE_COLS = 128
PAD_DIM = 448
CUT = ((0, 208), (208, 192))

CHUNK = 512
SLOT_COLS = NNEG + QMAX * BLOCK

learn_rate = 0.1
rel_rate = 0.02
weight = 1.0 / math.sqrt(NNEG)

F32 = jnp.float32
BF16 = jnp.bfloat16
VMEM = pltpu.VMEM
HBM = pl.ANY
SMEM = pltpu.SMEM
BY_COLS = (((1,), (1,)), ((), ()))


def on(p, e):
    return {"dom": p, "edge": e}


def remote(src, dst, send_sem, recv_sem, p, e):
    return pltpu.make_async_remote_copy(
        src_ref=src,
        dst_ref=dst,
        send_sem=send_sem,
        recv_sem=recv_sem,
        device_id=on(p, e),
        device_id_type=pl.DeviceIdType.MESH,
    )


def greet(devices):
    barrier = pltpu.get_barrier_semaphore()
    for p, e in devices:
        pl.semaphore_signal(
            barrier, inc=1, device_id=on(p, e), device_id_type=pl.DeviceIdType.MESH
        )
    pl.semaphore_wait(barrier, len(devices))


def split(x):
    high = x.astype(BF16)
    return high, (x - high.astype(F32)).astype(BF16)


def piece(k):
    rows = pl.ds(pl.multiple_of((k // 4) * PIECE_ROWS, 16), PIECE_ROWS)
    cols = pl.ds(pl.multiple_of((k % 4) * PIECE_COLS, 128), PIECE_COLS)
    return rows, cols


def pair_kernel(
    matching, table, state, shards_out, low_out, state_out,
    shards, low, own, landed_high, landed_low, picked, states,
    own_send, own_recv, pick_send, pick_recv, state_send, state_recv,
    right_send, right_recv, left_send, left_recv, core_send, core_recv, out_sem,
):
    p = lax.axis_index("dom")
    e = lax.axis_index("edge")
    z, core = e // 2, e % 2
    right = ((z + 1) % N_Z) * 2 + core
    left = ((z + N_Z - 1) % N_Z) * 2 + core
    sibling = z * 2 + 1 - core
    others = [(p + k) % N_DOM for k in range(1, N_DOM)]

    high_part, low_part = split(table[...])
    own[0, :DIM] = high_part
    own[1, :DIM] = low_part
    own[:, DIM:] = jnp.zeros((2, PAD_DIM - DIM, ROWS), BF16)
    states[p] = state[...]
    rows_p, cols_p = piece(p)

    greet([(t, e) for t in others] + [(p, right), (p, left), (p, sibling)])

    landed = (landed_high, landed_low)
    own_copies = [[], []]
    for part in range(2):
        for k, t in enumerate(others):
            rows, cols = piece(t)
            copy = remote(
                own.at[part, rows, cols], landed[part].at[p],
                own_send.at[part, k], own_recv.at[part, k], t, e,
            )
            copy.start()
            own_copies[part].append(copy)
        landed[part][p] = own[part, rows_p, cols_p]
    state_copies = []
    for k, t in enumerate(others):
        copy = remote(states.at[p], states.at[p], state_send.at[k], state_recv.at[k], t, e)
        copy.start()
        state_copies.append(copy)

    pick_copies = [[], []]

    def pick(part, target_ref):
        for copy in own_copies[part]:
            copy.wait_recv()
        for k, t in enumerate(others):
            picked[part, k] = landed[part][matching[t]]
            copy = remote(
                picked.at[part, k], target_ref.at[rows_p, cols_p],
                pick_send.at[part, k], pick_recv.at[part, k], t, e,
            )
            copy.start()
            pick_copies[part].append(copy)
        target_ref[rows_p, cols_p] = landed[part][matching[p]]

    pick(0, shards.at[e])
    pick(1, low)
    for copy in pick_copies[0]:
        copy.wait_recv()

    pending = []

    def go(step, half, to_right):
        source = ((z - step + N_Z) % N_Z if to_right else (z + step) % N_Z) * 2 + core
        start, size = CUT[half]
        ref = shards.at[source, pl.ds(start, size)]
        sems = (right_send, right_recv) if to_right else (left_send, left_recv)
        copy = remote(
            ref, ref, sems[0].at[step, half], sems[1].at[step, half],
            p, right if to_right else left,
        )
        copy.start()
        pending.append(copy)
        return copy

    across = []

    def cross(slot, source_z, half):
        start, size = CUT[half]
        ref = shards.at[source_z * 2 + core, pl.ds(start, size)]
        copy = remote(ref, ref, core_send.at[slot, half], core_recv.at[slot, half], p, sibling)
        copy.start()
        across.append(copy)

    flying = {}
    for half in range(2):
        flying[True, half] = go(0, half, True)
        flying[False, half] = go(0, half, False)
    for half in range(2):
        cross(0, z, half)
    for step in range(1, FAR + 1):
        for half in range(2):
            for to_right in (True, False):
                if step == FAR and to_right != (half == 0):
                    continue
                flying[to_right, half].wait_recv()
                source_z = (z - step + N_Z) % N_Z if to_right else (z + step) % N_Z
                if step < FAR - 1 or (step == FAR - 1 and to_right == (half == 0)):
                    flying[to_right, half] = go(step, half, to_right)
                if step == FAR:
                    slot = 2 * FAR - 1
                else:
                    slot = 2 * step - 1 if to_right else 2 * step
                cross(slot, source_z, half)

    for copy in own_copies[0] + own_copies[1] + pick_copies[0] + pending + across:
        copy.wait_send()
    for copy in pick_copies[1] + state_copies:
        copy.wait()
    for copy in across:
        copy.wait_recv()

    done = pltpu.make_async_copy(shards.at[:, pl.ds(0, DIM)], shards_out, out_sem.at[0])
    done.start()
    low_done = pltpu.make_async_copy(low.at[pl.ds(0, DIM)], low_out, out_sem.at[1])
    low_done.start()
    state_out[...] = states[matching[p]]
    done.wait()
    low_done.wait()


def pair(matching, table, state):
    dma = pltpu.SemaphoreType.DMA
    return pl.pallas_call(
        pair_kernel,
        out_shape=(
            jax.ShapeDtypeStruct((N_EDGE, DIM, ROWS), BF16),
            jax.ShapeDtypeStruct((DIM, ROWS), BF16),
            jax.ShapeDtypeStruct((1, ROWS), F32),
        ),
        in_specs=[
            pl.BlockSpec(memory_space=SMEM),
            pl.BlockSpec(memory_space=VMEM),
            pl.BlockSpec(memory_space=VMEM),
        ],
        out_specs=(
            pl.BlockSpec(memory_space=HBM),
            pl.BlockSpec(memory_space=HBM),
            pl.BlockSpec(memory_space=VMEM),
        ),
        scratch_shapes=[
            VMEM((N_EDGE, PAD_DIM, ROWS), BF16),
            VMEM((PAD_DIM, ROWS), BF16),
            VMEM((2, PAD_DIM, ROWS), BF16),
            VMEM((N_DOM, PIECE_ROWS, PIECE_COLS), BF16),
            VMEM((N_DOM, PIECE_ROWS, PIECE_COLS), BF16),
            VMEM((2, N_DOM - 1, PIECE_ROWS, PIECE_COLS), BF16),
            VMEM((N_DOM, 1, ROWS), F32),
            dma((2, N_DOM - 1)), dma((2, N_DOM - 1)),
            dma((2, N_DOM - 1)), dma((2, N_DOM - 1)),
            dma((N_DOM - 1,)), dma((N_DOM - 1,)),
            dma((FAR, 2)), dma((FAR, 2)), dma((FAR, 2)), dma((FAR, 2)),
            dma((N_Z, 2)), dma((N_Z, 2)),
            dma((2,)),
        ],
        compiler_params=pltpu.CompilerParams(
            collective_id=0, has_side_effects=True, vmem_limit_bytes=48 * 2**20
        ),
        name="pair_and_gather",
    )(matching, table, state)


def product(x_re, x_im, y_re, y_im):
    return x_re * y_re - x_im * y_im, x_re * y_im + x_im * y_re


def back(g_re, g_im, v_re, v_im):
    return g_re * v_re + g_im * v_im, g_im * v_re - g_re * v_im


def onehot(ids, count):
    places = lax.broadcasted_iota(jnp.int32, (count, ids.shape[1]), 0)
    return jnp.where(places == ids, 1.0, 0.0).astype(BF16)


def put_split(ref, re, im):
    x = jnp.concatenate([re, im], axis=0)
    high, low = split(x)
    ref[:DIM] = high
    ref[DIM:] = low


def both(x):
    return x[:HALF] + x[DIM : DIM + HALF], x[HALF:DIM] + x[DIM + HALF :]


def step_kernel(
    quotas, table, shards, low, relation, src_ids, dst_ids, rel_ids, neg_ids,
    dense_out, dst_out, src_out, rel_out,
    table2, part2, rel2, negs, negs_t, neg_grad, spread, src_acc, dst_acc, rel_acc,
):
    e = lax.axis_index("edge")
    ends = []
    total = 0
    for k in range(N_EDGE):
        total = total + quotas[0, k]
        ends.append(total)
    for j in range(QTOTAL):
        owner = 0
        for k in range(N_EDGE):
            owner = owner + jnp.where(ends[k] <= j, 1, 0)
        owner = jnp.minimum(owner, N_EDGE - 1)
        first = 0
        for k in range(N_EDGE):
            first = first + jnp.where(owner == k, ends[k] - quotas[0, k], 0)
        block = jnp.clip(owner * QMAX + j - first, 0, N_EDGE * QMAX - 1)
        rows = neg_ids[pl.ds(block, 1), :]
        found = jnp.dot(shards[owner], onehot(rows, ROWS), preferred_element_type=F32)
        negs[:, j * BLOCK : (j + 1) * BLOCK] = found.astype(BF16)
        negs_t[j * BLOCK : (j + 1) * BLOCK, :] = found.T.astype(BF16)

    table2[:DIM], table2[DIM:] = split(table[...])
    part2[:DIM] = shards[e]
    part2[DIM:] = low[...]
    rel2[:DIM], rel2[DIM:] = split(relation[...])
    neg_grad[...] = jnp.zeros_like(neg_grad)
    src_acc[...] = jnp.zeros_like(src_acc)
    dst_acc[...] = jnp.zeros_like(dst_acc)
    rel_acc[...] = jnp.zeros_like(rel_acc)

    @pl.loop(0, EDGES // CHUNK)
    def _(i):
        cols = pl.ds(pl.multiple_of(i * CHUNK, CHUNK), CHUNK)
        src_hot = onehot(src_ids[:, cols], ROWS)
        dst_hot = onehot(dst_ids[:, cols], ROWS)
        rel_hot = onehot(rel_ids[:, cols], NREL)
        s_re, s_im = both(jnp.dot(table2[...], src_hot, preferred_element_type=F32))
        d_re, d_im = both(jnp.dot(part2[...], dst_hot, preferred_element_type=F32))
        r_re, r_im = both(jnp.dot(rel2[...], rel_hot, preferred_element_type=F32))
        q_re, q_im = product(s_re, s_im, r_re, r_im)
        positive = jnp.sum(q_re * d_re + q_im * d_im, axis=0, keepdims=True)
        pos_coef = -jax.nn.sigmoid(-positive)
        query_b = jnp.concatenate([q_re, q_im], axis=0).astype(BF16)
        scores = jnp.dot(negs_t[...], query_b, preferred_element_type=F32)
        coef = (0.5 * weight + 0.5 * weight * jnp.tanh(0.5 * scores)).astype(BF16)
        neg_grad[:, :NNEG] += lax.dot_general(
            query_b, coef, BY_COLS, preferred_element_type=F32
        )
        g = jnp.dot(negs[...], coef, preferred_element_type=F32)
        g_re = pos_coef * d_re + g[:HALF]
        g_im = pos_coef * d_im + g[HALF:]
        put_split(spread, *back(g_re, g_im, r_re, r_im))
        src_acc[...] += lax.dot_general(spread[...], src_hot, BY_COLS, preferred_element_type=F32)
        put_split(spread, pos_coef * q_re, pos_coef * q_im)
        dst_acc[...] += lax.dot_general(spread[...], dst_hot, BY_COLS, preferred_element_type=F32)
        put_split(spread, *back(g_re, g_im, s_re, s_im))
        rel_acc[...] += lax.dot_general(spread[...], rel_hot, BY_COLS, preferred_element_type=F32)

    src_out[...] = src_acc[:DIM] + src_acc[DIM:]
    dst_out[...] = dst_acc[:DIM] + dst_acc[DIM:]
    rel_out[...] = (rel_acc[:DIM] + rel_acc[DIM:]).T

    for k in range(N_EDGE):
        first = ends[k] - quotas[0, k]
        parts = neg_grad[:, pl.ds(pl.multiple_of(first * BLOCK, BLOCK), QMAX * BLOCK)]
        hots = []
        for b in range(QMAX):
            hot = onehot(neg_ids[k * QMAX + b : k * QMAX + b + 1, :], ROWS)
            hots.append(jnp.where(b < quotas[0, k], hot, jnp.zeros_like(hot)))
        hot = jnp.concatenate(hots, axis=1)
        high, low_part = split(parts)
        summed = lax.dot_general(high, hot, BY_COLS, preferred_element_type=F32)
        summed += lax.dot_general(low_part, hot, BY_COLS, preferred_element_type=F32)
        dense_out[k] = summed


def step(quotas, table, shards, low, relation, src_ids, dst_ids, rel_ids, neg_ids):
    vmem = pl.BlockSpec(memory_space=VMEM)
    return pl.pallas_call(
        step_kernel,
        out_shape=(
            jax.ShapeDtypeStruct((N_EDGE, DIM, ROWS), F32),
            jax.ShapeDtypeStruct((DIM, ROWS), F32),
            jax.ShapeDtypeStruct((DIM, ROWS), F32),
            jax.ShapeDtypeStruct((NREL, DIM), F32),
        ),
        in_specs=[pl.BlockSpec(memory_space=SMEM)] + [vmem] * 8,
        out_specs=(vmem,) * 4,
        scratch_shapes=[
            VMEM((2 * DIM, ROWS), BF16),
            VMEM((2 * DIM, ROWS), BF16),
            VMEM((2 * DIM, NREL), BF16),
            VMEM((DIM, NNEG), BF16),
            VMEM((NNEG, DIM), BF16),
            VMEM((DIM, SLOT_COLS), F32),
            VMEM((2 * DIM, CHUNK), BF16),
            VMEM((2 * DIM, ROWS), F32),
            VMEM((2 * DIM, ROWS), F32),
            VMEM((2 * DIM, NREL), F32),
        ],
        compiler_params=pltpu.CompilerParams(vmem_limit_bytes=60 * 2**20),
        name="edges",
    )(quotas, table, shards, low, relation, src_ids, dst_ids, rel_ids, neg_ids)


def adagrad(table, state, grad):
    new_state = state + jnp.sum(grad * grad, axis=0, keepdims=True) * (1.0 / DIM)
    return table - learn_rate * grad / jnp.sqrt(new_state), new_state


def finish_kernel(
    dense, dst_grad, src_grad, rel_grad, src_table, src_state, part_high, part_low, part_state,
    relation, src_out, src_state_out, dst_out, dst_state_out, relation_out,
    give, taken, comb, sent_right, sent_left, got_right, got_left, rel_rows, rel_sums, rel_all,
    core_send, core_recv, right_send, right_recv, left_send, left_recv,
    rel_send, rel_recv,
):
    p = lax.axis_index("dom")
    e = lax.axis_index("edge")
    z, core = e // 2, e % 2
    right = ((z + 1) % N_Z) * 2 + core
    left = ((z + N_Z - 1) % N_Z) * 2 + core
    sibling = z * 2 + 1 - core
    dom_others = [(p + k) % N_DOM for k in range(1, N_DOM)]
    edge_others = [(e + k) % N_EDGE for k in range(1, N_EDGE)]
    order = [FAR]
    for d in range(FAR - 1, 0, -1):
        order += [d, N_Z - d]
    order.append(0)

    for d in order:
        give[d] = dense[((z + d) % N_Z) * 2 + 1 - core].astype(BF16)

    greet([(t, e) for t in dom_others] + [(p, t) for t in edge_others])

    core_copies = {}
    for d in order:
        copy = remote(give.at[d], taken.at[d], core_send.at[d], core_recv.at[d], p, sibling)
        copy.start()
        core_copies[d] = copy

    rel_copies = []
    first = []
    for k, t in enumerate(dom_others):
        copy = remote(
            rel_grad.at[t], rel_rows.at[p], rel_send.at[0, k], rel_recv.at[0, k], t, e
        )
        copy.start()
        first.append(copy)
    rel_rows[p] = rel_grad[p]

    ring = {}
    for d in order:
        core_copies[d].wait_recv()
        comb[d] = dense[((z + d) % N_Z) * 2 + core] + taken[d].astype(F32)

    copies = []
    for step in range(FAR):
        d = FAR - step
        for half in range(2):
            start, size = CUT[half]
            rows = pl.ds(start, size)
            for to_right in (True, False):
                if step == 0 and to_right != (half == 0):
                    continue
                place = d if to_right else (N_Z - d) % N_Z
                value = comb[place, rows]
                came = step >= 2 or (step == 1 and to_right == (half == 0))
                got = got_right if to_right else got_left
                sent = sent_right if to_right else sent_left
                if came:
                    ring[to_right, half].wait_recv()
                    value = value + got[step - 1, rows].astype(F32)
                sent[step, rows] = value.astype(BF16)
                send, recv = (right_send, right_recv) if to_right else (left_send, left_recv)
                copy = remote(
                    sent.at[step, rows], got.at[step, rows],
                    send.at[step, half], recv.at[step, half], p, right if to_right else left,
                )
                copy.start()
                ring[to_right, half] = copy
                copies.append(copy)

    for copy in first:
        copy.wait_recv()
    rel_sums[e] = jnp.sum(rel_rows[...], axis=0)
    second = []
    for k, t in enumerate(edge_others):
        copy = remote(
            rel_sums.at[e], rel_sums.at[e], rel_send.at[1, k], rel_recv.at[1, k], p, t
        )
        copy.start()
        second.append(copy)

    src_out[...], src_state_out[...] = adagrad(src_table[...], src_state[...], src_grad[...])

    for copy in second:
        copy.wait_recv()
    rel_all[p] = jnp.sum(rel_sums[...], axis=0)
    third = []
    for k, t in enumerate(dom_others):
        copy = remote(rel_all.at[p], rel_all.at[p], rel_send.at[2, k], rel_recv.at[2, k], t, e)
        copy.start()
        third.append(copy)

    for half in range(2):
        ring[True, half].wait_recv()
        ring[False, half].wait_recv()
    grad = dst_grad[...] + comb[0]
    grad = grad + got_right[FAR - 1].astype(F32) + got_left[FAR - 1].astype(F32)
    part = part_high[...].astype(F32) + part_low[...].astype(F32)
    dst_out[...], dst_state_out[...] = adagrad(part, part_state[...], grad)

    for copy in third:
        copy.wait_recv()
    relation_out[...] = relation[...] - rel_rate * rel_all[...]

    for copy in copies + first + second + third + list(core_copies.values()):
        copy.wait_send()


def finish(dense, dst_grad, src_grad, rel_grad, src_table, src_state, high, low, state, relation):
    dma = pltpu.SemaphoreType.DMA
    vmem = pl.BlockSpec(memory_space=VMEM)
    return pl.pallas_call(
        finish_kernel,
        out_shape=(
            jax.ShapeDtypeStruct((DIM, ROWS), F32),
            jax.ShapeDtypeStruct((1, ROWS), F32),
            jax.ShapeDtypeStruct((DIM, ROWS), F32),
            jax.ShapeDtypeStruct((1, ROWS), F32),
            jax.ShapeDtypeStruct((NREL, 1, DIM), F32),
        ),
        in_specs=[vmem] * 10,
        out_specs=(vmem,) * 5,
        scratch_shapes=[
            VMEM((N_Z, DIM, ROWS), BF16),
            VMEM((N_Z, DIM, ROWS), BF16),
            VMEM((N_Z, DIM, ROWS), F32),
            VMEM((FAR, DIM, ROWS), BF16),
            VMEM((FAR, DIM, ROWS), BF16),
            VMEM((FAR, DIM, ROWS), BF16),
            VMEM((FAR, DIM, ROWS), BF16),
            VMEM((N_DOM, 1, DIM), F32),
            VMEM((N_EDGE, 1, DIM), F32),
            VMEM((NREL, 1, DIM), F32),
            dma((N_Z,)), dma((N_Z,)),
            dma((FAR, 2)), dma((FAR, 2)), dma((FAR, 2)), dma((FAR, 2)),
            dma((3, N_DOM - 1)), dma((3, N_DOM - 1)),
        ],
        compiler_params=pltpu.CompilerParams(
            collective_id=1, has_side_effects=True, vmem_limit_bytes=60 * 2**20
        ),
        name="reduce_and_update",
    )(dense, dst_grad, src_grad, rel_grad, src_table, src_state, high, low, state, relation)


def shards(
    src_table,
    src_state,
    dst_table,
    dst_state,
    relation,
    edge_src,
    edge_dst,
    edge_rel,
    matching,
    neg_rows,
    quotas,
):
    gathered, low, state = pair(matching, dst_table, dst_state.reshape(1, ROWS))
    dense, dst_grad, src_grad, rel_grad = step(
        quotas,
        src_table,
        gathered,
        low,
        relation,
        edge_src.reshape(1, EDGES),
        edge_dst.reshape(1, EDGES),
        edge_rel.reshape(1, EDGES),
        neg_rows.reshape(N_EDGE * QMAX, BLOCK),
    )
    high = lax.dynamic_index_in_dim(gathered, lax.axis_index("edge"), 0, False)
    src_out, src_state_out, dst_out, dst_state_out, relation_out = finish(
        dense,
        dst_grad,
        src_grad,
        rel_grad.reshape(NREL, 1, DIM),
        src_table,
        src_state.reshape(1, ROWS),
        high,
        low,
        state,
        relation.T.reshape(NREL, 1, DIM),
    )
    return (
        src_out,
        src_state_out.reshape(ROWS),
        dst_out,
        dst_state_out.reshape(ROWS),
        relation_out.reshape(NREL, DIM).T,
    )


def solution(mesh):
    in_specs = (
        P(None, ("dom", "edge")),
        P(("dom", "edge")),
        P(None, ("dom", "edge")),
        P(("dom", "edge")),
        P(),
        P(("dom", "edge")),
        P(("dom", "edge")),
        P(("dom", "edge")),
        P(),
        P(("dom", "edge"), None, None),
        P(("dom", "edge"), None),
    )
    out_specs = (
        P(None, ("dom", "edge")),
        P(("dom", "edge")),
        P(None, ("dom", "edge")),
        P(("dom", "edge")),
        P(),
    )
    return jax.shard_map(shards, mesh=mesh, in_specs=in_specs, out_specs=out_specs, check_vma=False)
```

```python
import math

import jax
import jax.numpy as jnp
from jax import lax
from jax.experimental import pallas as pl
from jax.experimental.pallas import tpu as pltpu
from jax.sharding import PartitionSpec as P

DIM = 400
HALF = 200
NREL = 16
BLOCK = 128
QMAX = 2
QTOTAL = 12
NNEG = 1536
ROWS = 512
EDGES = 4096
N_DOM = 16
N_EDGE = 16
N_Z = 8
FAR = N_Z // 2
DISTANCES = (4, 3, 5, 2, 6, 1, 7, 0)
NEAR_FROM = 512

PIECE_ROWS = 112
PIECE_COLS = 128
PAD_DIM = 448
CUT = ((0, 208), (208, 192))

CHUNK = 512
N_CHUNK = EDGES // CHUNK

learn_rate = 0.1
rel_rate = 0.02
weight = 1.0 / math.sqrt(NNEG)

F32 = jnp.float32
BF16 = jnp.bfloat16
VMEM = pltpu.VMEM
HBM = pl.ANY
SMEM = pltpu.SMEM
BY_COLS = (((1,), (1,)), ((), ()))


def on(p, e):
    return {"dom": p, "edge": e}


def remote(src, dst, send_sem, recv_sem, p, e):
    return pltpu.make_async_remote_copy(
        src_ref=src,
        dst_ref=dst,
        send_sem=send_sem,
        recv_sem=recv_sem,
        device_id=on(p, e),
        device_id_type=pl.DeviceIdType.MESH,
    )


def greet(devices):
    barrier = pltpu.get_barrier_semaphore()
    for p, e in devices:
        pl.semaphore_signal(
            barrier, inc=1, device_id=on(p, e), device_id_type=pl.DeviceIdType.MESH
        )
    pl.semaphore_wait(barrier, len(devices))


def split(x):
    high = x.astype(BF16)
    return high, (x - high.astype(F32)).astype(BF16)


def piece(k):
    rows = pl.ds(pl.multiple_of((k // 4) * PIECE_ROWS, 16), PIECE_ROWS)
    cols = pl.ds(pl.multiple_of((k % 4) * PIECE_COLS, 128), PIECE_COLS)
    return rows, cols


def product(x_re, x_im, y_re, y_im):
    return x_re * y_re - x_im * y_im, x_re * y_im + x_im * y_re


def back(g_re, g_im, v_re, v_im):
    return g_re * v_re + g_im * v_im, g_im * v_re - g_re * v_im


def onehot(ids, count):
    places = lax.broadcasted_iota(jnp.int32, (count, ids.shape[1]), 0)
    return jnp.where(places == ids, 1.0, 0.0).astype(BF16)


def put_split(ref, re, im):
    x = jnp.concatenate([re, im], axis=0)
    high, low = split(x)
    ref[:DIM] = high
    ref[DIM:] = low


def both(x):
    return x[:HALF] + x[DIM : DIM + HALF], x[HALF:DIM] + x[DIM + HALF :]


def plan_kernel(quotas, neg_rows, plan, slots):
    e = lax.axis_index("edge")
    z, core = e // 2, e % 2
    owners, ends = [], []
    total = 0
    for g in range(N_EDGE):
        owner = ((z + DISTANCES[g // 2]) % N_Z) * 2 + (core if g % 2 == 0 else 1 - core)
        plan[2 * QTOTAL + g] = total
        total = total + quotas[0, owner]
        owners.append(owner)
        ends.append(total)
    for j in range(QTOTAL):
        owner = owners[0]
        first = 0
        for g in range(1, N_EDGE):
            owner = jnp.where(ends[g - 1] <= j, owners[g], owner)
            first = jnp.where(ends[g - 1] <= j, ends[g - 1], first)
        plan[j] = owner
        plan[QTOTAL + j] = owner * QMAX + jnp.clip(j - first, 0, QMAX - 1)
    lanes = lax.broadcasted_iota(jnp.int32, (1, QMAX * BLOCK), 1)
    for k in range(N_EDGE):
        live = jnp.where(lanes < quotas[0, k] * BLOCK, neg_rows[k : k + 1], -1)
        for b in range(QMAX):
            slots[k * QMAX + b] = live[:, b * BLOCK : (b + 1) * BLOCK]


def make_plan(quotas, neg_rows):
    smem = pl.BlockSpec(memory_space=SMEM)
    vmem = pl.BlockSpec(memory_space=VMEM)
    return pl.pallas_call(
        plan_kernel,
        out_shape=(
            jax.ShapeDtypeStruct((2 * QTOTAL + N_EDGE,), jnp.int32),
            jax.ShapeDtypeStruct((N_EDGE * QMAX, 1, BLOCK), jnp.int32),
        ),
        in_specs=[smem, vmem],
        out_specs=(smem, vmem),
        name="plan",
    )(quotas, neg_rows)


def kernel(
    matching, plan, table, state, src_table_hbm, src_state, relation,
    src_ids, dst_ids, rel_ids, slots,
    src_step_out, src_state_out, part_out, dst_step_out, dst_state_out, rel_out,
    shards, low, own, landed_high, landed_low, picked, states, src_table,
    table2, part2, rel2, query_b, hold, coefs, negs, negs_t, neg_grad, spread,
    src_acc, dst_acc, rel_acc, taken, got_right, got_left,
    rel_mine, rel_rows, rel_sums,
    own_send, own_recv, pick_send, pick_recv, state_send, state_recv,
    right_send, right_recv, left_send, left_recv, core_send, core_recv,
    give_send, give_recv, down_send, down_recv, up_send, up_recv,
    rel_send, rel_recv, local_sem,
):
    p = lax.axis_index("dom")
    e = lax.axis_index("edge")
    z, core = e // 2, e % 2
    right = ((z + 1) % N_Z) * 2 + core
    left = ((z + N_Z - 1) % N_Z) * 2 + core
    sibling = z * 2 + 1 - core
    others = [(p + k) % N_DOM for k in range(1, N_DOM)]
    edge_others = [(e + k) % N_EDGE for k in range(1, N_EDGE)]
    rows_p, cols_p = piece(p)
    sent = []

    fetch = pltpu.make_async_copy(src_table_hbm, src_table, local_sem.at[0])
    fetch.start()
    own[0, :DIM], own[1, :DIM] = split(table[...])
    own[:, DIM:] = jnp.zeros((2, PAD_DIM - DIM, ROWS), BF16)
    states[p] = state[...]

    greet([(t, e) for t in others] + [(p, t) for t in edge_others])

    landed = (landed_high, landed_low)

    def spread_pieces(part):
        copies = []
        for k, t in enumerate(others):
            rows, cols = piece(t)
            copy = remote(
                own.at[part, rows, cols], landed[part].at[p],
                own_send.at[part, k], own_recv.at[part, k], t, e,
            )
            copy.start()
            copies.append(copy)
        landed[part][p] = own[part, rows_p, cols_p]
        sent.extend(copies)
        return copies

    def pick(part, came, target_ref):
        for copy in came:
            copy.wait_recv()
        copies = []
        for k, t in enumerate(others):
            picked[part, k] = landed[part][matching[t]]
            copy = remote(
                picked.at[part, k], target_ref.at[rows_p, cols_p],
                pick_send.at[part, k], pick_recv.at[part, k], t, e,
            )
            copy.start()
            copies.append(copy)
        target_ref[rows_p, cols_p] = landed[part][matching[p]]
        sent.extend(copies)
        return copies

    came_high = spread_pieces(0)

    rel_acc[...] = jnp.zeros_like(rel_acc)
    src_acc[...] = jnp.zeros_like(src_acc)
    dst_acc[...] = jnp.zeros_like(dst_acc)
    neg_grad[...] = jnp.zeros_like(neg_grad)
    rel2[:DIM], rel2[DIM:] = split(relation[...].T)
    fetch.wait()
    table2[:DIM], table2[DIM:] = split(src_table[...])

    def chunk_cols(i):
        return pl.ds(pl.multiple_of(i * CHUNK, CHUNK), CHUNK)

    def source_rows(cols):
        src_hot = onehot(src_ids[:, cols], ROWS)
        rel_hot = onehot(rel_ids[:, cols], NREL)
        s_re, s_im = both(jnp.dot(table2[...], src_hot, preferred_element_type=F32))
        r_re, r_im = both(jnp.dot(rel2[...], rel_hot, preferred_element_type=F32))
        return src_hot, rel_hot, s_re, s_im, r_re, r_im

    def queries(first, last):
        @pl.loop(first, last)
        def _(i):
            cols = chunk_cols(i)
            _, _, s_re, s_im, r_re, r_im = source_rows(cols)
            q_re, q_im = product(s_re, s_im, r_re, r_im)
            hold[:HALF, cols] = q_re
            hold[HALF:, cols] = q_im
            query_b[:, cols] = jnp.concatenate([q_re, q_im], axis=0).astype(BF16)

    def positives(first, last):
        @pl.loop(first, last)
        def _(i):
            cols = chunk_cols(i)
            dst_hot = onehot(dst_ids[:, cols], ROWS)
            d_re, d_im = both(jnp.dot(part2[...], dst_hot, preferred_element_type=F32))
            q_re, q_im = hold[:HALF, cols], hold[HALF:, cols]
            positive = jnp.sum(q_re * d_re + q_im * d_im, axis=0, keepdims=True)
            pos_coef = -jax.nn.sigmoid(-positive)
            put_split(spread, pos_coef * q_re, pos_coef * q_im)
            dst_acc[...] += lax.dot_general(
                spread[...], dst_hot, BY_COLS, preferred_element_type=F32
            )
            hold[:HALF, cols] = pos_coef * d_re
            hold[HALF:, cols] = pos_coef * d_im

    came_high = pick(0, came_high, shards.at[e])
    queries(0, 2)
    for copy in came_high:
        copy.wait_recv()

    flying = {}

    def go(step, half, to_right):
        source = ((z - step + N_Z) % N_Z if to_right else (z + step) % N_Z) * 2 + core
        start, size = CUT[half]
        ref = shards.at[source, pl.ds(start, size)]
        sems = (right_send, right_recv) if to_right else (left_send, left_recv)
        copy = remote(
            ref, ref, sems[0].at[step, half], sems[1].at[step, half],
            p, right if to_right else left,
        )
        copy.start()
        sent.append(copy)
        flying[to_right, half] = copy

    across = []

    def cross(slot, source_z, half):
        start, size = CUT[half]
        ref = shards.at[source_z * 2 + core, pl.ds(start, size)]
        copy = remote(ref, ref, core_send.at[slot, half], core_recv.at[slot, half], p, sibling)
        copy.start()
        across.append(copy)

    def forward(step, half):
        for to_right in (True, False):
            if step == FAR and to_right != (half == 0):
                continue
            flying[to_right, half].wait_recv()
            source_z = (z - step + N_Z) % N_Z if to_right else (z + step) % N_Z
            if step < FAR - 1 or (step == FAR - 1 and to_right == (half == 0)):
                go(step, half, to_right)
            if step == FAR:
                slot = 2 * FAR - 1
            else:
                slot = 2 * step - 1 if to_right else 2 * step
            cross(slot, source_z, half)

    for half in range(2):
        go(0, half, True)
        go(0, half, False)
    for half in range(2):
        cross(0, z, half)
    came_low = spread_pieces(1)
    state_copies = []
    for k, t in enumerate(others):
        copy = remote(states.at[p], states.at[p], state_send.at[k], state_recv.at[k], t, e)
        copy.start()
        state_copies.append(copy)
    sent.extend(state_copies)

    queries(2, 5)
    came_low = pick(1, came_low, low)
    forward(1, 0)
    queries(5, 8)
    forward(1, 1)
    part2[:DIM] = shards[e, :DIM]
    for copy in came_low:
        copy.wait_recv()
    part2[DIM:] = low[:DIM]
    part_done = pltpu.make_async_copy(part2, part_out, local_sem.at[1])
    part_done.start()
    positives(0, 2)
    forward(2, 0)
    positives(2, 4)
    forward(2, 1)
    positives(4, 6)
    forward(3, 0)
    positives(6, 7)
    forward(3, 1)
    positives(7, 8)
    forward(4, 0)
    forward(4, 1)
    for copy in across:
        copy.wait()

    for j in range(QTOTAL):
        hot = onehot(slots[plan[QTOTAL + j]], ROWS)
        found = jnp.dot(shards[plan[j], :DIM], hot, preferred_element_type=F32)
        negs[:, j * BLOCK : (j + 1) * BLOCK] = found.astype(BF16)
        negs_t[j * BLOCK : (j + 1) * BLOCK, :] = found.T.astype(BF16)

    def negatives(first, last):
        @pl.loop(0, N_CHUNK)
        def _(i):
            cols = chunk_cols(i)
            scores = jnp.dot(
                negs_t[first:last], query_b[:, cols], preferred_element_type=F32
            )
            coef = (0.5 * weight + 0.5 * weight * jnp.tanh(0.5 * scores)).astype(BF16)
            coefs[first:last, cols] = coef
            added = lax.dot_general(
                query_b[:, cols], coef, BY_COLS, preferred_element_type=F32
            )
            for j in range(first // BLOCK, last // BLOCK):
                at = j * BLOCK - first
                neg_grad[j] += added[:, at : at + BLOCK]

    for copy in sent:
        copy.wait_send()
    sent.clear()

    give_copies = {}

    def dense(g):
        first = plan[2 * QTOTAL + g]
        owner = ((z + DISTANCES[g // 2]) % N_Z) * 2 + (core if g % 2 == 0 else 1 - core)
        parts = jnp.concatenate([neg_grad[first + b] for b in range(QMAX)], axis=1)
        ids = jnp.concatenate([slots[owner * QMAX + b] for b in range(QMAX)], axis=1)
        hot = onehot(ids, ROWS)
        high, low_part = split(parts)
        summed = lax.dot_general(high, hot, BY_COLS, preferred_element_type=F32)
        return summed + lax.dot_general(low_part, hot, BY_COLS, preferred_element_type=F32)

    def contribute(at):
        d = DISTANCES[at]
        shards[N_Z + d, :DIM] = dense(2 * at + 1).astype(BF16)
        copy = remote(
            shards.at[N_Z + d, pl.ds(0, DIM)], taken.at[d],
            give_send.at[d], give_recv.at[d], p, sibling,
        )
        copy.start()
        sent.append(copy)
        give_copies[d] = copy
        shards[d, :DIM] = dense(2 * at).astype(BF16)

    joined = set()
    ring = {}

    def reduce_step(step, half):
        d = FAR - step
        start, size = CUT[half]
        rows = pl.ds(start, size)
        for to_right in (True, False):
            if step == 0 and to_right != (half == 0):
                continue
            place = d if to_right else (N_Z - d) % N_Z
            if place not in joined:
                give_copies[place].wait_recv()
                joined.add(place)
            value = shards[place, rows].astype(F32) + taken[place, rows].astype(F32)
            got = got_right if to_right else got_left
            if step >= 2 or (step == 1 and to_right == (half == 0)):
                ring[to_right, half].wait_recv()
                value = value + got[step - 1, rows].astype(F32)
            shards[place, rows] = value.astype(BF16)
            send, recv = (down_send, down_recv) if to_right else (up_send, up_recv)
            copy = remote(
                shards.at[place, rows], got.at[step, rows],
                send.at[step, half], recv.at[step, half], p, right if to_right else left,
            )
            copy.start()
            ring[to_right, half] = copy
            sent.append(copy)

    def query_grads(first, last):
        @pl.loop(first, last)
        def _(i):
            cols = chunk_cols(i)
            src_hot, rel_hot, s_re, s_im, r_re, r_im = source_rows(cols)
            g = jnp.dot(negs[...], coefs[:, cols], preferred_element_type=F32)
            g_re = hold[:HALF, cols] + g[:HALF]
            g_im = hold[HALF:, cols] + g[HALF:]
            put_split(spread, *back(g_re, g_im, r_re, r_im))
            src_acc[...] += lax.dot_general(
                spread[...], src_hot, BY_COLS, preferred_element_type=F32
            )
            put_split(spread, *back(g_re, g_im, s_re, s_im))
            rel_acc[...] += lax.dot_general(
                spread[...], rel_hot, BY_COLS, preferred_element_type=F32
            )

    negatives(0, NEAR_FROM)
    contribute(0)
    reduce_step(0, 0)
    reduce_step(0, 1)
    negatives(NEAR_FROM, NNEG)
    contribute(1)
    contribute(2)
    reduce_step(1, 0)
    reduce_step(1, 1)
    contribute(3)
    contribute(4)
    query_grads(0, 2)
    reduce_step(2, 0)
    query_grads(2, 3)
    contribute(5)
    contribute(6)
    reduce_step(2, 1)
    query_grads(3, 5)
    contribute(7)
    reduce_step(3, 0)
    query_grads(5, 7)
    reduce_step(3, 1)
    query_grads(7, 8)

    rel_grad = (rel_acc[:DIM] + rel_acc[DIM:]).T
    for r in range(NREL):
        rel_mine[r] = rel_grad[r : r + 1]
    first_copies = []
    for k, t in enumerate(others):
        copy = remote(
            rel_mine.at[t], rel_rows.at[p], rel_send.at[0, k], rel_recv.at[0, k], t, e
        )
        copy.start()
        first_copies.append(copy)
    rel_rows[p] = rel_mine[p]

    new_state = src_state[...]
    grad = src_acc[:DIM] + src_acc[DIM:]
    src_step, src_state_out[...] = adagrad(new_state, grad)
    src_acc[:DIM] = src_step
    src_done = pltpu.make_async_copy(src_acc.at[pl.ds(0, DIM)], src_step_out, local_sem.at[2])
    src_done.start()

    for copy in first_copies:
        copy.wait_recv()
    rel_sums[e] = jnp.sum(rel_rows[...], axis=0)
    second_copies = []
    for k, t in enumerate(edge_others):
        copy = remote(
            rel_sums.at[e], rel_sums.at[e], rel_send.at[1, k], rel_recv.at[1, k], p, t
        )
        copy.start()
        second_copies.append(copy)

    dst_acc[:DIM] = dst_acc[:DIM] + dst_acc[DIM:]
    for copy in state_copies:
        copy.wait_recv()
    part_state = states[matching[p]]
    give_copies[0].wait_recv()
    dst_acc[:DIM] = dst_acc[:DIM] + shards[0, :DIM].astype(F32) + taken[0].astype(F32)

    for copy in second_copies:
        copy.wait_recv()
    rel_out[p] = jnp.sum(rel_sums[...], axis=0)
    third_copies = []
    for k, t in enumerate(others):
        copy = remote(rel_out.at[p], rel_out.at[p], rel_send.at[2, k], rel_recv.at[2, k], t, e)
        copy.start()
        third_copies.append(copy)

    for half in range(2):
        ring[True, half].wait_recv()
        ring[False, half].wait_recv()
    grad = dst_acc[:DIM] + got_right[FAR - 1].astype(F32) + got_left[FAR - 1].astype(F32)
    dst_step, dst_state_out[...] = adagrad(part_state, grad)
    dst_acc[:DIM] = dst_step
    dst_done = pltpu.make_async_copy(dst_acc.at[pl.ds(0, DIM)], dst_step_out, local_sem.at[3])
    dst_done.start()

    for copy in third_copies:
        copy.wait_recv()
    for copy in sent + first_copies + second_copies + third_copies:
        copy.wait_send()
    part_done.wait()
    src_done.wait()
    dst_done.wait()


def adagrad(state, grad):
    new_state = state + jnp.sum(grad * grad, axis=0, keepdims=True) * (1.0 / DIM)
    return learn_rate * grad / jnp.sqrt(new_state), new_state


def run(*args):
    dma = pltpu.SemaphoreType.DMA
    vmem = pl.BlockSpec(memory_space=VMEM)
    smem = pl.BlockSpec(memory_space=SMEM)
    hbm = pl.BlockSpec(memory_space=HBM)
    return pl.pallas_call(
        kernel,
        out_shape=(
            jax.ShapeDtypeStruct((DIM, ROWS), F32),
            jax.ShapeDtypeStruct((1, ROWS), F32),
            jax.ShapeDtypeStruct((2 * DIM, ROWS), BF16),
            jax.ShapeDtypeStruct((DIM, ROWS), F32),
            jax.ShapeDtypeStruct((1, ROWS), F32),
            jax.ShapeDtypeStruct((NREL, 1, DIM), F32),
        ),
        in_specs=[smem, smem, vmem, vmem, hbm] + [vmem] * 6,
        out_specs=(hbm, vmem, hbm, hbm, vmem, vmem),
        scratch_shapes=[
            VMEM((N_EDGE, PAD_DIM, ROWS), BF16),
            VMEM((PAD_DIM, ROWS), BF16),
            VMEM((2, PAD_DIM, ROWS), BF16),
            VMEM((N_DOM, PIECE_ROWS, PIECE_COLS), BF16),
            VMEM((N_DOM, PIECE_ROWS, PIECE_COLS), BF16),
            VMEM((2, N_DOM - 1, PIECE_ROWS, PIECE_COLS), BF16),
            VMEM((N_DOM, 1, ROWS), F32),
            VMEM((DIM, ROWS), F32),
            VMEM((2 * DIM, ROWS), BF16),
            VMEM((2 * DIM, ROWS), BF16),
            VMEM((2 * DIM, NREL), BF16),
            VMEM((DIM, EDGES), BF16),
            VMEM((DIM, EDGES), F32),
            VMEM((NNEG, EDGES), BF16),
            VMEM((DIM, NNEG), BF16),
            VMEM((NNEG, DIM), BF16),
            VMEM((QTOTAL + QMAX, DIM, BLOCK), F32),
            VMEM((2 * DIM, CHUNK), BF16),
            VMEM((2 * DIM, ROWS), F32),
            VMEM((2 * DIM, ROWS), F32),
            VMEM((2 * DIM, NREL), F32),
            VMEM((N_Z, DIM, ROWS), BF16),
            VMEM((FAR, DIM, ROWS), BF16),
            VMEM((FAR, DIM, ROWS), BF16),
            VMEM((NREL, 1, DIM), F32),
            VMEM((N_DOM, 1, DIM), F32),
            VMEM((N_EDGE, 1, DIM), F32),
            dma((2, N_DOM - 1)), dma((2, N_DOM - 1)),
            dma((2, N_DOM - 1)), dma((2, N_DOM - 1)),
            dma((N_DOM - 1,)), dma((N_DOM - 1,)),
            dma((FAR, 2)), dma((FAR, 2)), dma((FAR, 2)), dma((FAR, 2)),
            dma((N_Z, 2)), dma((N_Z, 2)),
            dma((N_Z,)), dma((N_Z,)),
            dma((FAR, 2)), dma((FAR, 2)), dma((FAR, 2)), dma((FAR, 2)),
            dma((3, N_DOM - 1)), dma((3, N_DOM - 1)),
            dma((4,)),
        ],
        compiler_params=pltpu.CompilerParams(
            collective_id=0, has_side_effects=True, vmem_limit_bytes=60 * 2**20
        ),
        name="bucket_step",
    )(*args)


def shards(
    src_table,
    src_state,
    dst_table,
    dst_state,
    relation,
    edge_src,
    edge_dst,
    edge_rel,
    matching,
    neg_rows,
    quotas,
):
    plan, slots = make_plan(quotas, neg_rows.reshape(N_EDGE, QMAX * BLOCK))
    src_step, src_state_out, part, dst_step, dst_state_out, rel_total = run(
        matching,
        plan,
        dst_table,
        dst_state.reshape(1, ROWS),
        src_table,
        src_state.reshape(1, ROWS),
        relation.T,
        edge_src.reshape(1, EDGES),
        edge_dst.reshape(1, EDGES),
        edge_rel.reshape(1, EDGES),
        slots,
    )
    return (
        src_table - src_step,
        src_state_out.reshape(ROWS),
        part[:DIM].astype(F32) + part[DIM:].astype(F32) - dst_step,
        dst_state_out.reshape(ROWS),
        relation - rel_rate * rel_total.reshape(NREL, DIM).T,
    )


def solution(mesh):
    in_specs = (
        P(None, ("dom", "edge")),
        P(("dom", "edge")),
        P(None, ("dom", "edge")),
        P(("dom", "edge")),
        P(),
        P(("dom", "edge")),
        P(("dom", "edge")),
        P(("dom", "edge")),
        P(),
        P(("dom", "edge"), None, None),
        P(("dom", "edge"), None),
    )
    out_specs = (
        P(None, ("dom", "edge")),
        P(("dom", "edge")),
        P(None, ("dom", "edge")),
        P(("dom", "edge")),
        P(),
    )
    return jax.shard_map(shards, mesh=mesh, in_specs=in_specs, out_specs=out_specs, check_vma=False)
```

```python
import math

import jax
import jax.numpy as jnp
from jax import lax
from jax.experimental import pallas as pl
from jax.experimental.pallas import tpu as pltpu
from jax.sharding import PartitionSpec as P

DIM = 400
HALF = 200
NREL = 16
BLOCK = 128
QMAX = 2
QTOTAL = 12
NNEG = 1536
ROWS = 512
EDGES = 4096
N_DOM = 16
N_EDGE = 16
N_Z = 8
FAR = N_Z // 2
DISTANCES = (0, 7, 1, 6, 2, 5, 3, 4)
NEAR_BLOCKS = 8

PAIRED = ((0, 0, 48), (0, 192, 64), (1, 0, 112))
PIECE_COLS = 128
PAD_DIM = 448
CUT = ((0, 192), (192, 208))

CHUNK = 512
N_CHUNK = EDGES // CHUNK

learn_rate = 0.1
rel_rate = 0.02
weight = 1.0 / math.sqrt(NNEG)

F32 = jnp.float32
BF16 = jnp.bfloat16
VMEM = pltpu.VMEM
HBM = pl.ANY
SMEM = pltpu.SMEM
BY_COLS = (((1,), (1,)), ((), ()))


def on(p, e):
    return {"dom": p, "edge": e}


def remote(src, dst, send_sem, recv_sem, p, e):
    return pltpu.make_async_remote_copy(
        src_ref=src,
        dst_ref=dst,
        send_sem=send_sem,
        recv_sem=recv_sem,
        device_id=on(p, e),
        device_id_type=pl.DeviceIdType.MESH,
    )


def greet(devices):
    barrier = pltpu.get_barrier_semaphore()
    for p, e in devices:
        pl.semaphore_signal(
            barrier, inc=1, device_id=on(p, e), device_id_type=pl.DeviceIdType.MESH
        )
    pl.semaphore_wait(barrier, len(devices))


def split(x):
    high = x.astype(BF16)
    return high, (x - high.astype(F32)).astype(BF16)


def piece(k, part):
    _, start, size = PAIRED[part]
    rows = pl.ds(pl.multiple_of(start + (k // 4) * size, 16), size)
    cols = pl.ds(pl.multiple_of((k % 4) * PIECE_COLS, 128), PIECE_COLS)
    return rows, cols


def product(x_re, x_im, y_re, y_im):
    return x_re * y_re - x_im * y_im, x_re * y_im + x_im * y_re


def back(g_re, g_im, v_re, v_im):
    return g_re * v_re + g_im * v_im, g_im * v_re - g_re * v_im


def onehot(ids, count):
    places = lax.broadcasted_iota(jnp.int32, (count, ids.shape[1]), 0)
    return jnp.where(places == ids, 1.0, 0.0).astype(BF16)


def put_split(ref, re, im):
    x = jnp.concatenate([re, im], axis=0)
    high, low = split(x)
    ref[:DIM] = high
    ref[DIM:] = low


def both(x):
    return x[:HALF] + x[DIM : DIM + HALF], x[HALF:DIM] + x[DIM + HALF :]


def plan_kernel(quotas, neg_rows, plan, slots, near_ids, far_ids):
    e = lax.axis_index("edge")
    z, core = e // 2, e % 2
    lanes = lax.broadcasted_iota(jnp.int32, (1, QMAX * BLOCK), 1)
    for k in range(N_EDGE):
        live = jnp.where(lanes < quotas[0, k] * BLOCK, neg_rows[k : k + 1], -1)
        for b in range(QMAX):
            slots[k * QMAX + b] = live[:, b * BLOCK : (b + 1) * BLOCK]
    owners, ends = [], []
    total = 0
    for g in range(N_EDGE):
        owner = ((z + DISTANCES[g // 2]) % N_Z) * 2 + (core if g % 2 == 0 else 1 - core)
        plan[2 * QTOTAL + g] = total
        total = total + quotas[0, owner]
        owners.append(owner)
        ends.append(total)
    nearer = ends[N_EDGE - QMAX - 1]
    for j in range(QTOTAL):
        owner = owners[0]
        first = 0
        for g in range(1, N_EDGE):
            owner = jnp.where(ends[g - 1] <= j, owners[g], owner)
            first = jnp.where(ends[g - 1] <= j, ends[g - 1], first)
        rows = slots[owner * QMAX + jnp.clip(j - first, 0, QMAX - 1)]
        plan[j] = jnp.where(j < nearer, owner, e)
        plan[QTOTAL + j] = jnp.where(j < nearer, 0, owner % 2)
        near_ids[j] = jnp.where(j < nearer, rows, -1)
        if j >= NEAR_BLOCKS:
            far_ids[j - NEAR_BLOCKS] = jnp.where(j < nearer, -1, rows)


def make_plan(quotas, neg_rows):
    smem = pl.BlockSpec(memory_space=SMEM)
    vmem = pl.BlockSpec(memory_space=VMEM)
    return pl.pallas_call(
        plan_kernel,
        out_shape=(
            jax.ShapeDtypeStruct((2 * QTOTAL + N_EDGE,), jnp.int32),
            jax.ShapeDtypeStruct((N_EDGE * QMAX, 1, BLOCK), jnp.int32),
            jax.ShapeDtypeStruct((QTOTAL, 1, BLOCK), jnp.int32),
            jax.ShapeDtypeStruct((QTOTAL - NEAR_BLOCKS, 1, BLOCK), jnp.int32),
        ),
        in_specs=[smem, vmem],
        out_specs=(smem, vmem, vmem, vmem),
        name="plan",
    )(quotas, neg_rows)


def kernel(
    matching, plan, table, state, src_table_hbm, src_state, relation,
    src_ids, dst_ids, rel_ids, slots, near_ids, far_ids,
    src_step_out, src_state_out, part_out, dst_step_out, dst_state_out, rel_out,
    shards, far, low, own, landed_a, landed_b, landed_low, picked_a, picked_b, picked_low,
    states, src_table,
    table2, part2, rel2, query_b, hold, coefs, negs, negs_t, neg_grad, spread,
    src_acc, dst_acc, rel_acc, taken, got_right, got_left,
    rel_mine, rel_rows, rel_sums,
    own_send, own_recv, pick_send, pick_recv, state_send, state_recv,
    right_send, right_recv, left_send, left_recv, core_send, core_recv,
    give_send, give_recv, down_send, down_recv, up_send, up_recv,
    rel_send, rel_recv, local_sem,
):
    p = lax.axis_index("dom")
    e = lax.axis_index("edge")
    z, core = e // 2, e % 2
    right = ((z + 1) % N_Z) * 2 + core
    left = ((z + N_Z - 1) % N_Z) * 2 + core
    sibling = z * 2 + 1 - core
    others = [(p + k) % N_DOM for k in range(1, N_DOM)]
    edge_others = [(e + k) % N_EDGE for k in range(1, N_EDGE)]
    sent = []

    fetch = pltpu.make_async_copy(src_table_hbm, src_table, local_sem.at[0])
    fetch.start()
    own[0, :DIM], own[1, :DIM] = split(table[...])
    own[:, DIM:] = jnp.zeros((2, PAD_DIM - DIM, ROWS), BF16)
    states[p] = state[...]

    greet([(t, e) for t in others] + [(p, t) for t in edge_others])

    landed = (landed_a, landed_b, landed_low)
    picked = (picked_a, picked_b, picked_low)

    def spread_pieces(part):
        copies = []
        for k, t in enumerate(others):
            rows, cols = piece(t, part)
            copy = remote(
                own.at[PAIRED[part][0], rows, cols], landed[part].at[p],
                own_send.at[part, k], own_recv.at[part, k], t, e,
            )
            copy.start()
            copies.append(copy)
        rows, cols = piece(p, part)
        landed[part][p] = own[PAIRED[part][0], rows, cols]
        sent.extend(copies)
        return copies

    def pick(part, came, target_ref):
        for copy in came:
            copy.wait_recv()
        rows, cols = piece(p, part)
        copies = []
        for k, t in enumerate(others):
            picked[part][k] = landed[part][matching[t]]
            copy = remote(
                picked[part].at[k], target_ref.at[rows, cols],
                pick_send.at[part, k], pick_recv.at[part, k], t, e,
            )
            copy.start()
            copies.append(copy)
        target_ref[rows, cols] = landed[part][matching[p]]
        sent.extend(copies)
        return copies

    came_a = spread_pieces(0)
    rel_acc[...] = jnp.zeros_like(rel_acc)
    src_acc[...] = jnp.zeros_like(src_acc)
    dst_acc[...] = jnp.zeros_like(dst_acc)
    rel2[:DIM], rel2[DIM:] = split(relation[...].T)
    picks_a = pick(0, came_a, shards.at[e])
    came_b = spread_pieces(1)
    neg_grad[...] = jnp.zeros_like(neg_grad)
    fetch.wait()
    table2[:DIM], table2[DIM:] = split(src_table[...])

    def chunk_cols(i):
        return pl.ds(pl.multiple_of(i * CHUNK, CHUNK), CHUNK)

    def source_rows(cols):
        src_hot = onehot(src_ids[:, cols], ROWS)
        rel_hot = onehot(rel_ids[:, cols], NREL)
        s_re, s_im = both(jnp.dot(table2[...], src_hot, preferred_element_type=F32))
        r_re, r_im = both(jnp.dot(rel2[...], rel_hot, preferred_element_type=F32))
        return src_hot, rel_hot, s_re, s_im, r_re, r_im

    def queries(first, last):
        @pl.loop(first, last)
        def _(i):
            cols = chunk_cols(i)
            _, _, s_re, s_im, r_re, r_im = source_rows(cols)
            q_re, q_im = product(s_re, s_im, r_re, r_im)
            hold[:HALF, cols] = q_re
            hold[HALF:, cols] = q_im
            query_b[:, cols] = jnp.concatenate([q_re, q_im], axis=0).astype(BF16)

    def positives(first, last):
        @pl.loop(first, last)
        def _(i):
            cols = chunk_cols(i)
            dst_hot = onehot(dst_ids[:, cols], ROWS)
            d_re, d_im = both(jnp.dot(part2[...], dst_hot, preferred_element_type=F32))
            q_re, q_im = hold[:HALF, cols], hold[HALF:, cols]
            positive = jnp.sum(q_re * d_re + q_im * d_im, axis=0, keepdims=True)
            pos_coef = -jax.nn.sigmoid(-positive)
            put_split(spread, pos_coef * q_re, pos_coef * q_im)
            dst_acc[...] += lax.dot_general(
                spread[...], dst_hot, BY_COLS, preferred_element_type=F32
            )
            hold[:HALF, cols] = pos_coef * d_re
            hold[HALF:, cols] = pos_coef * d_im

    flying = {}

    def go(step, half, to_right):
        source = ((z - step + N_Z) % N_Z if to_right else (z + step) % N_Z) * 2 + core
        start, size = CUT[half]
        ref = shards.at[source, pl.ds(start, size)]
        target = far.at[core, pl.ds(start, size)] if step == FAR - 1 else ref
        sems = (right_send, right_recv) if to_right else (left_send, left_recv)
        copy = remote(
            ref, target, sems[0].at[step, half], sems[1].at[step, half],
            p, right if to_right else left,
        )
        copy.start()
        sent.append(copy)
        flying[to_right, half] = copy

    across = []

    def cross(slot, source_z, half):
        start, size = CUT[half]
        held, at = (far, core) if slot == 2 * FAR - 1 else (shards, source_z * 2 + core)
        ref = held.at[at, pl.ds(start, size)]
        copy = remote(ref, ref, core_send.at[slot, half], core_recv.at[slot, half], p, sibling)
        copy.start()
        across.append(copy)

    def forward(step, half):
        for to_right in (True, False):
            if step == FAR and to_right != (half == 0):
                continue
            flying[to_right, half].wait_recv()
            source_z = (z - step + N_Z) % N_Z if to_right else (z + step) % N_Z
            if step < FAR - 1 or (step == FAR - 1 and to_right == (half == 0)):
                go(step, half, to_right)
            if step == FAR:
                slot = 2 * FAR - 1
            else:
                slot = 2 * step - 1 if to_right else 2 * step
            cross(slot, source_z, half)

    def begin(half, picks):
        for copy in picks:
            copy.wait_recv()
        go(0, half, True)
        go(0, half, False)
        cross(0, z, half)

    begin(0, picks_a)
    picks_b = pick(1, came_b, shards.at[e])
    queries(0, 2)
    begin(1, picks_b)
    came_low = spread_pieces(2)
    state_copies = []
    for k, t in enumerate(others):
        copy = remote(states.at[p], states.at[p], state_send.at[k], state_recv.at[k], t, e)
        copy.start()
        state_copies.append(copy)
    sent.extend(state_copies)
    forward(1, 0)
    queries(2, 5)
    picks_low = pick(2, came_low, low)
    forward(1, 1)
    queries(5, 8)
    forward(2, 0)
    part2[:DIM] = shards[e, :DIM]
    for copy in picks_low:
        copy.wait_recv()
    part2[DIM:] = low[:DIM]
    part_done = pltpu.make_async_copy(part2, part_out, local_sem.at[1])
    part_done.start()
    positives(0, 2)
    forward(2, 1)
    positives(2, 5)
    forward(3, 0)
    positives(5, 8)
    forward(3, 1)

    def gather(j):
        hot = onehot(near_ids[j], ROWS)
        found = jnp.dot(shards[plan[j], :DIM], hot, preferred_element_type=F32)
        if j >= NEAR_BLOCKS:
            hot = onehot(far_ids[j - NEAR_BLOCKS], ROWS)
            found += jnp.dot(far[plan[QTOTAL + j]], hot, preferred_element_type=F32)
        negs[:, j * BLOCK : (j + 1) * BLOCK] = found.astype(BF16)
        negs_t[j * BLOCK : (j + 1) * BLOCK, :] = found.T.astype(BF16)

    def negatives(first, last, chunk_from=0, chunk_to=N_CHUNK):
        @pl.loop(chunk_from, chunk_to)
        def _(i):
            cols = chunk_cols(i)
            scores = jnp.dot(
                negs_t[first:last], query_b[:, cols], preferred_element_type=F32
            )
            coef = (0.5 * weight + 0.5 * weight * jnp.tanh(0.5 * scores)).astype(BF16)
            coefs[first:last, cols] = coef
            added = lax.dot_general(
                query_b[:, cols], coef, BY_COLS, preferred_element_type=F32
            )
            for j in range(first // BLOCK, last // BLOCK):
                at = j * BLOCK - first
                neg_grad[j] += added[:, at : at + BLOCK]

    for copy in across:
        copy.wait()
    across.clear()
    for j in range(NEAR_BLOCKS):
        gather(j)
    negatives(0, 512, 0, 4)
    forward(4, 0)
    forward(4, 1)
    negatives(0, 512, 4, 8)
    for copy in across:
        copy.wait()
    for j in range(NEAR_BLOCKS, QTOTAL):
        gather(j)

    for copy in sent:
        copy.wait_send()
    sent.clear()

    give_copies = {}

    def dense(g):
        first = plan[2 * QTOTAL + g]
        owner = ((z + DISTANCES[g // 2]) % N_Z) * 2 + (core if g % 2 == 0 else 1 - core)
        parts = jnp.concatenate([neg_grad[first + b] for b in range(QMAX)], axis=1)
        ids = jnp.concatenate([slots[owner * QMAX + b] for b in range(QMAX)], axis=1)
        hot = onehot(ids, ROWS)
        high, low_part = split(parts)
        summed = lax.dot_general(high, hot, BY_COLS, preferred_element_type=F32)
        return summed + lax.dot_general(low_part, hot, BY_COLS, preferred_element_type=F32)

    def contribute(at):
        at = N_Z - 1 - at
        d = DISTANCES[at]
        shards[N_Z + d, :DIM] = dense(2 * at + 1).astype(BF16)
        copy = remote(
            shards.at[N_Z + d, pl.ds(0, DIM)], taken.at[d],
            give_send.at[d], give_recv.at[d], p, sibling,
        )
        copy.start()
        sent.append(copy)
        give_copies[d] = copy
        shards[d, :DIM] = dense(2 * at).astype(BF16)

    joined = set()
    ring = {}

    def reduce_step(step, half, ways=(True, False)):
        d = FAR - step
        start, size = CUT[half]
        rows = pl.ds(start, size)
        for to_right in ways:
            if step == 0 and to_right != (half == 0):
                continue
            place = d if to_right else (N_Z - d) % N_Z
            if place not in joined:
                give_copies[place].wait_recv()
                joined.add(place)
            value = shards[place, rows].astype(F32) + taken[place, rows].astype(F32)
            got = got_right if to_right else got_left
            if step >= 2 or (step == 1 and to_right == (half == 0)):
                ring[to_right, half].wait_recv()
                value = value + got[step - 1, rows].astype(F32)
            shards[place, rows] = value.astype(BF16)
            send, recv = (down_send, down_recv) if to_right else (up_send, up_recv)
            copy = remote(
                shards.at[place, rows], got.at[step, rows],
                send.at[step, half], recv.at[step, half], p, right if to_right else left,
            )
            copy.start()
            ring[to_right, half] = copy
            sent.append(copy)

    def query_grads(first, last):
        @pl.loop(first, last)
        def _(i):
            cols = chunk_cols(i)
            src_hot, rel_hot, s_re, s_im, r_re, r_im = source_rows(cols)
            g = jnp.dot(negs[...], coefs[:, cols], preferred_element_type=F32)
            g_re = hold[:HALF, cols] + g[:HALF]
            g_im = hold[HALF:, cols] + g[HALF:]
            put_split(spread, *back(g_re, g_im, r_re, r_im))
            src_acc[...] += lax.dot_general(
                spread[...], src_hot, BY_COLS, preferred_element_type=F32
            )
            put_split(spread, *back(g_re, g_im, s_re, s_im))
            rel_acc[...] += lax.dot_general(
                spread[...], rel_hot, BY_COLS, preferred_element_type=F32
            )

    negatives(1024, 1536)
    contribute(0)
    reduce_step(0, 0)
    reduce_step(0, 1)
    negatives(512, 1024)
    contribute(1)
    contribute(2)
    for way in (True, False):
        for half in range(2):
            reduce_step(1, half, (way,))
    contribute(3)
    contribute(4)
    query_grads(0, 2)
    reduce_step(2, 0)
    query_grads(2, 3)
    contribute(5)
    contribute(6)
    reduce_step(2, 1)
    query_grads(3, 5)
    contribute(7)
    reduce_step(3, 0)
    query_grads(5, 7)
    reduce_step(3, 1)
    query_grads(7, 8)

    rel_grad = (rel_acc[:DIM] + rel_acc[DIM:]).T
    for r in range(NREL):
        rel_mine[r] = rel_grad[r : r + 1]
    first_copies = []
    for k, t in enumerate(others):
        copy = remote(
            rel_mine.at[t], rel_rows.at[p], rel_send.at[0, k], rel_recv.at[0, k], t, e
        )
        copy.start()
        first_copies.append(copy)
    rel_rows[p] = rel_mine[p]

    new_state = src_state[...]
    grad = src_acc[:DIM] + src_acc[DIM:]
    src_step, src_state_out[...] = adagrad(new_state, grad)
    src_acc[:DIM] = src_step
    src_done = pltpu.make_async_copy(src_acc.at[pl.ds(0, DIM)], src_step_out, local_sem.at[2])
    src_done.start()

    for copy in first_copies:
        copy.wait_recv()
    rel_sums[e] = jnp.sum(rel_rows[...], axis=0)
    second_copies = []
    for k, t in enumerate(edge_others):
        copy = remote(
            rel_sums.at[e], rel_sums.at[e], rel_send.at[1, k], rel_recv.at[1, k], p, t
        )
        copy.start()
        second_copies.append(copy)

    dst_acc[:DIM] = dst_acc[:DIM] + dst_acc[DIM:]
    for copy in state_copies:
        copy.wait_recv()
    part_state = states[matching[p]]
    give_copies[0].wait_recv()
    dst_acc[:DIM] = dst_acc[:DIM] + shards[0, :DIM].astype(F32) + taken[0].astype(F32)

    for copy in second_copies:
        copy.wait_recv()
    rel_out[p] = jnp.sum(rel_sums[...], axis=0)
    third_copies = []
    for k, t in enumerate(others):
        copy = remote(rel_out.at[p], rel_out.at[p], rel_send.at[2, k], rel_recv.at[2, k], t, e)
        copy.start()
        third_copies.append(copy)

    for half in range(2):
        ring[True, half].wait_recv()
        ring[False, half].wait_recv()
    grad = dst_acc[:DIM] + got_right[FAR - 1].astype(F32) + got_left[FAR - 1].astype(F32)
    dst_step, dst_state_out[...] = adagrad(part_state, grad)
    dst_acc[:DIM] = dst_step
    dst_done = pltpu.make_async_copy(dst_acc.at[pl.ds(0, DIM)], dst_step_out, local_sem.at[3])
    dst_done.start()

    for copy in third_copies:
        copy.wait_recv()
    for copy in sent + first_copies + second_copies + third_copies:
        copy.wait_send()
    part_done.wait()
    src_done.wait()
    dst_done.wait()


def adagrad(state, grad):
    new_state = state + jnp.sum(grad * grad, axis=0, keepdims=True) * (1.0 / DIM)
    return learn_rate * grad / jnp.sqrt(new_state), new_state


def run(*args):
    dma = pltpu.SemaphoreType.DMA
    vmem = pl.BlockSpec(memory_space=VMEM)
    smem = pl.BlockSpec(memory_space=SMEM)
    hbm = pl.BlockSpec(memory_space=HBM)
    return pl.pallas_call(
        kernel,
        out_shape=(
            jax.ShapeDtypeStruct((DIM, ROWS), F32),
            jax.ShapeDtypeStruct((1, ROWS), F32),
            jax.ShapeDtypeStruct((2 * DIM, ROWS), BF16),
            jax.ShapeDtypeStruct((DIM, ROWS), F32),
            jax.ShapeDtypeStruct((1, ROWS), F32),
            jax.ShapeDtypeStruct((NREL, 1, DIM), F32),
        ),
        in_specs=[smem, smem, vmem, vmem, hbm] + [vmem] * 8,
        out_specs=(hbm, vmem, hbm, hbm, vmem, vmem),
        scratch_shapes=[
            VMEM((N_EDGE, PAD_DIM, ROWS), BF16),
            VMEM((2, DIM, ROWS), BF16),
            VMEM((PAD_DIM, ROWS), BF16),
            VMEM((2, PAD_DIM, ROWS), BF16),
            *(VMEM((N_DOM, size, PIECE_COLS), BF16) for _, _, size in PAIRED),
            *(VMEM((N_DOM - 1, size, PIECE_COLS), BF16) for _, _, size in PAIRED),
            VMEM((N_DOM, 1, ROWS), F32),
            VMEM((DIM, ROWS), F32),
            VMEM((2 * DIM, ROWS), BF16),
            VMEM((2 * DIM, ROWS), BF16),
            VMEM((2 * DIM, NREL), BF16),
            VMEM((DIM, EDGES), BF16),
            VMEM((DIM, EDGES), F32),
            VMEM((NNEG, EDGES), BF16),
            VMEM((DIM, NNEG), BF16),
            VMEM((NNEG, DIM), BF16),
            VMEM((QTOTAL + QMAX, DIM, BLOCK), F32),
            VMEM((2 * DIM, CHUNK), BF16),
            VMEM((2 * DIM, ROWS), F32),
            VMEM((2 * DIM, ROWS), F32),
            VMEM((2 * DIM, NREL), F32),
            VMEM((N_Z, DIM, ROWS), BF16),
            VMEM((FAR, DIM, ROWS), BF16),
            VMEM((FAR, DIM, ROWS), BF16),
            VMEM((NREL, 1, DIM), F32),
            VMEM((N_DOM, 1, DIM), F32),
            VMEM((N_EDGE, 1, DIM), F32),
            dma((3, N_DOM - 1)), dma((3, N_DOM - 1)),
            dma((3, N_DOM - 1)), dma((3, N_DOM - 1)),
            dma((N_DOM - 1,)), dma((N_DOM - 1,)),
            dma((FAR, 2)), dma((FAR, 2)), dma((FAR, 2)), dma((FAR, 2)),
            dma((N_Z, 2)), dma((N_Z, 2)),
            dma((N_Z,)), dma((N_Z,)),
            dma((FAR, 2)), dma((FAR, 2)), dma((FAR, 2)), dma((FAR, 2)),
            dma((3, N_DOM - 1)), dma((3, N_DOM - 1)),
            dma((4,)),
        ],
        compiler_params=pltpu.CompilerParams(
            collective_id=0, has_side_effects=True, vmem_limit_bytes=60 * 2**20
        ),
        name="bucket_step",
    )(*args)


def finish_kernel(
    src_table, src_step, src_state, part, dst_step, dst_state, relation, rel_total,
    src_out, src_state_out, dst_out, dst_state_out, relation_out,
):
    src_out[...] = src_table[...] - src_step[...]
    src_state_out[...] = src_state[...]
    dst_out[...] = part[:DIM].astype(F32) + part[DIM:].astype(F32) - dst_step[...]
    dst_state_out[...] = dst_state[...]
    for r in range(NREL):
        relation_out[r : r + 1] = relation[r : r + 1] - rel_rate * rel_total[r]


def finish(*args):
    vmem = pl.BlockSpec(memory_space=VMEM)
    return pl.pallas_call(
        finish_kernel,
        out_shape=(
            jax.ShapeDtypeStruct((DIM, ROWS), F32),
            jax.ShapeDtypeStruct((1, ROWS), F32),
            jax.ShapeDtypeStruct((DIM, ROWS), F32),
            jax.ShapeDtypeStruct((1, ROWS), F32),
            jax.ShapeDtypeStruct((NREL, DIM), F32),
        ),
        in_specs=[vmem] * 8,
        out_specs=(vmem,) * 5,
        compiler_params=pltpu.CompilerParams(vmem_limit_bytes=60 * 2**20),
        name="finish",
    )(*args)


def shards(
    src_table,
    src_state,
    dst_table,
    dst_state,
    relation,
    edge_src,
    edge_dst,
    edge_rel,
    matching,
    neg_rows,
    quotas,
):
    plan, slots, near_ids, far_ids = make_plan(quotas, neg_rows.reshape(N_EDGE, QMAX * BLOCK))
    src_step, src_state_out, part, dst_step, dst_state_out, rel_total = run(
        matching,
        plan,
        dst_table,
        dst_state.reshape(1, ROWS),
        src_table,
        src_state.reshape(1, ROWS),
        relation.T,
        edge_src.reshape(1, EDGES),
        edge_dst.reshape(1, EDGES),
        edge_rel.reshape(1, EDGES),
        slots,
        near_ids,
        far_ids,
    )
    src_out, src_state_out, dst_out, dst_state_out, relation_out = finish(
        src_table, src_step, src_state_out, part, dst_step, dst_state_out, relation.T, rel_total
    )
    return (
        src_out,
        src_state_out.reshape(ROWS),
        dst_out,
        dst_state_out.reshape(ROWS),
        relation_out.T,
    )


def solution(mesh):
    in_specs = (
        P(None, ("dom", "edge")),
        P(("dom", "edge")),
        P(None, ("dom", "edge")),
        P(("dom", "edge")),
        P(),
        P(("dom", "edge")),
        P(("dom", "edge")),
        P(("dom", "edge")),
        P(),
        P(("dom", "edge"), None, None),
        P(("dom", "edge"), None),
    )
    out_specs = (
        P(None, ("dom", "edge")),
        P(("dom", "edge")),
        P(None, ("dom", "edge")),
        P(("dom", "edge")),
        P(),
    )
    return jax.shard_map(shards, mesh=mesh, in_specs=in_specs, out_specs=out_specs, check_vma=False)
```

```python
import math

import jax
import jax.numpy as jnp
from jax import lax
from jax.experimental import pallas as pl
from jax.experimental.pallas import tpu as pltpu
from jax.sharding import PartitionSpec as P

DIM = 400
HALF = 200
NREL = 16
BLOCK = 128
QMAX = 2
QTOTAL = 12
NNEG = 1536
ROWS = 512
EDGES = 4096
N_DOM = 16
N_EDGE = 16
N_Z = 8
FAR = N_Z // 2
DISTANCES = (0, 7, 1, 6, 2, 5, 3, 4)
NEAR_BLOCKS = 8
EARLY = 512

PAIRED = ((0, 0, 48), (0, 192, 64), (1, 0, 112))
PIECE_COLS = 128
PAD_DIM = 448
CUT = ((0, 192), (192, 208))

CHUNK = 512
N_CHUNK = EDGES // CHUNK

learn_rate = 0.1
rel_rate = 0.02
weight = 1.0 / math.sqrt(NNEG)

F32 = jnp.float32
BF16 = jnp.bfloat16
VMEM = pltpu.VMEM
HBM = pl.ANY
SMEM = pltpu.SMEM
BY_COLS = (((1,), (1,)), ((), ()))


def on(p, e):
    return {"dom": p, "edge": e}


def remote(src, dst, send_sem, recv_sem, p, e):
    return pltpu.make_async_remote_copy(
        src_ref=src,
        dst_ref=dst,
        send_sem=send_sem,
        recv_sem=recv_sem,
        device_id=on(p, e),
        device_id_type=pl.DeviceIdType.MESH,
    )


def greet(devices):
    barrier = pltpu.get_barrier_semaphore()
    for p, e in devices:
        pl.semaphore_signal(
            barrier, inc=1, device_id=on(p, e), device_id_type=pl.DeviceIdType.MESH
        )
    pl.semaphore_wait(barrier, len(devices))


def split(x):
    high = x.astype(BF16)
    return high, (x - high.astype(F32)).astype(BF16)


def piece(k, part):
    _, start, size = PAIRED[part]
    rows = pl.ds(pl.multiple_of(start + (k // 4) * size, 16), size)
    cols = pl.ds(pl.multiple_of((k % 4) * PIECE_COLS, 128), PIECE_COLS)
    return rows, cols


def product(x_re, x_im, y_re, y_im):
    return x_re * y_re - x_im * y_im, x_re * y_im + x_im * y_re


def back(g_re, g_im, v_re, v_im):
    return g_re * v_re + g_im * v_im, g_im * v_re - g_re * v_im


def onehot(ids, count):
    places = lax.broadcasted_iota(jnp.int32, (count, ids.shape[1]), 0)
    return jnp.where(places == ids, 1.0, 0.0).astype(BF16)


def put_split(ref, re, im):
    x = jnp.concatenate([re, im], axis=0)
    high, low = split(x)
    ref[:DIM] = high
    ref[DIM:] = low


def both(x):
    return x[:HALF] + x[DIM : DIM + HALF], x[HALF:DIM] + x[DIM + HALF :]


def plan_kernel(quotas, neg_rows, plan, slots, near_ids, far_ids):
    e = lax.axis_index("edge")
    z, core = e // 2, e % 2
    lanes = lax.broadcasted_iota(jnp.int32, (1, QMAX * BLOCK), 1)
    for k in range(N_EDGE):
        live = jnp.where(lanes < quotas[0, k] * BLOCK, neg_rows[k : k + 1], -1)
        for b in range(QMAX):
            slots[k * QMAX + b] = live[:, b * BLOCK : (b + 1) * BLOCK]
    owners, ends = [], []
    total = 0
    for g in range(N_EDGE):
        owner = ((z + DISTANCES[g // 2]) % N_Z) * 2 + (core if g % 2 == 0 else 1 - core)
        plan[2 * QTOTAL + g] = total
        total = total + quotas[0, owner]
        owners.append(owner)
        ends.append(total)
    nearer = ends[N_EDGE - QMAX - 1]
    for j in range(QTOTAL):
        owner = owners[0]
        first = 0
        for g in range(1, N_EDGE):
            owner = jnp.where(ends[g - 1] <= j, owners[g], owner)
            first = jnp.where(ends[g - 1] <= j, ends[g - 1], first)
        rows = slots[owner * QMAX + jnp.clip(j - first, 0, QMAX - 1)]
        plan[j] = jnp.where(j < nearer, owner, e)
        plan[QTOTAL + j] = jnp.where(j < nearer, 0, owner % 2)
        near_ids[j] = jnp.where(j < nearer, rows, -1)
        if j >= NEAR_BLOCKS:
            far_ids[j - NEAR_BLOCKS] = jnp.where(j < nearer, -1, rows)


def make_plan(quotas, neg_rows):
    smem = pl.BlockSpec(memory_space=SMEM)
    vmem = pl.BlockSpec(memory_space=VMEM)
    return pl.pallas_call(
        plan_kernel,
        out_shape=(
            jax.ShapeDtypeStruct((2 * QTOTAL + N_EDGE,), jnp.int32),
            jax.ShapeDtypeStruct((N_EDGE * QMAX, 1, BLOCK), jnp.int32),
            jax.ShapeDtypeStruct((QTOTAL, 1, BLOCK), jnp.int32),
            jax.ShapeDtypeStruct((QTOTAL - NEAR_BLOCKS, 1, BLOCK), jnp.int32),
        ),
        in_specs=[smem, vmem],
        out_specs=(smem, vmem, vmem, vmem),
        name="plan",
    )(quotas, neg_rows)


def kernel(
    matching, plan, table, state, src_table_hbm, src_state, relation,
    src_ids, dst_ids, rel_ids, slots, near_ids, far_ids,
    src_step_out, src_state_out, part_out, dst_step_out, dst_state_out, rel_out,
    shards, far, low, own, landed_a, landed_b, landed_low, picked_a, picked_b, picked_low,
    states, source,
    table2, part2, rel2, query_b, hold, coefs, negs, negs_t, neg_grad, spread,
    src_acc, dst_acc, rel_acc, taken, got_right, got_left,
    rel_mine, rel_rows, rel_sums,
    own_send, own_recv, pick_send, pick_recv, state_send, state_recv,
    right_send, right_recv, left_send, left_recv, core_send, core_recv,
    give_send, give_recv, down_send, down_recv, up_send, up_recv,
    rel_send, rel_recv, local_sem,
):
    p = lax.axis_index("dom")
    e = lax.axis_index("edge")
    z, core = e // 2, e % 2
    right = ((z + 1) % N_Z) * 2 + core
    left = ((z + N_Z - 1) % N_Z) * 2 + core
    sibling = z * 2 + 1 - core
    others = [(p + k) % N_DOM for k in range(1, N_DOM)]
    edge_others = [(e + k) % N_EDGE for k in range(1, N_EDGE)]
    sent = []

    fetch = pltpu.make_async_copy(src_table_hbm, src_acc.at[pl.ds(0, DIM)], local_sem.at[0])
    fetch.start()
    own[0, :DIM], own[1, :DIM] = split(table[...])
    own[:, DIM:] = jnp.zeros((2, PAD_DIM - DIM, ROWS), BF16)
    states[p] = state[...]

    greet([(t, e) for t in others] + [(p, t) for t in edge_others])

    landed = (landed_a, landed_b, landed_low)
    picked = (picked_a, picked_b, picked_low)

    def spread_pieces(part):
        copies = []
        for k, t in enumerate(others):
            rows, cols = piece(t, part)
            copy = remote(
                own.at[PAIRED[part][0], rows, cols], landed[part].at[p],
                own_send.at[part, k], own_recv.at[part, k], t, e,
            )
            copy.start()
            copies.append(copy)
        rows, cols = piece(p, part)
        landed[part][p] = own[PAIRED[part][0], rows, cols]
        sent.extend(copies)
        return copies

    def pick(part, came, target_ref):
        for copy in came:
            copy.wait_recv()
        rows, cols = piece(p, part)
        copies = []
        for k, t in enumerate(others):
            picked[part][k] = landed[part][matching[t]]
            copy = remote(
                picked[part].at[k], target_ref.at[rows, cols],
                pick_send.at[part, k], pick_recv.at[part, k], t, e,
            )
            copy.start()
            copies.append(copy)
        target_ref[rows, cols] = landed[part][matching[p]]
        sent.extend(copies)
        return copies

    came_a = spread_pieces(0)
    rel_acc[...] = jnp.zeros_like(rel_acc)
    dst_acc[...] = jnp.zeros_like(dst_acc)
    rel2[:DIM], rel2[DIM:] = split(relation[...].T)
    picks_a = pick(0, came_a, shards.at[e])
    came_b = spread_pieces(1)
    neg_grad[...] = jnp.zeros_like(neg_grad)
    fetch.wait()
    table2[:DIM], table2[DIM:] = split(src_acc[:DIM])
    src_acc[...] = jnp.zeros_like(src_acc)

    def chunk_cols(i):
        return pl.ds(pl.multiple_of(i * CHUNK, CHUNK), CHUNK)

    def relation_rows(cols):
        rel_hot = onehot(rel_ids[:, cols], NREL)
        r_re, r_im = both(jnp.dot(rel2[...], rel_hot, preferred_element_type=F32))
        return rel_hot, r_re, r_im

    def queries(first, last):
        @pl.loop(first, last)
        def _(i):
            cols = chunk_cols(i)
            src_hot = onehot(src_ids[:, cols], ROWS)
            s_re, s_im = both(jnp.dot(table2[...], src_hot, preferred_element_type=F32))
            _, r_re, r_im = relation_rows(cols)
            source[:HALF, cols] = s_re
            source[HALF:, cols] = s_im
            q_re, q_im = product(s_re, s_im, r_re, r_im)
            hold[:HALF, cols] = q_re
            hold[HALF:, cols] = q_im
            query_b[:, cols] = jnp.concatenate([q_re, q_im], axis=0).astype(BF16)

    def positives(first, last):
        @pl.loop(first, last)
        def _(i):
            cols = chunk_cols(i)
            dst_hot = onehot(dst_ids[:, cols], ROWS)
            d_re, d_im = both(jnp.dot(part2[...], dst_hot, preferred_element_type=F32))
            q_re, q_im = hold[:HALF, cols], hold[HALF:, cols]
            positive = jnp.sum(q_re * d_re + q_im * d_im, axis=0, keepdims=True)
            pos_coef = -jax.nn.sigmoid(-positive)
            put_split(spread, pos_coef * q_re, pos_coef * q_im)
            dst_acc[...] += lax.dot_general(
                spread[...], dst_hot, BY_COLS, preferred_element_type=F32
            )
            hold[:HALF, cols] = pos_coef * d_re
            hold[HALF:, cols] = pos_coef * d_im

    flying = {}

    def go(step, half, to_right):
        source = ((z - step + N_Z) % N_Z if to_right else (z + step) % N_Z) * 2 + core
        start, size = CUT[half]
        ref = shards.at[source, pl.ds(start, size)]
        target = far.at[core, pl.ds(start, size)] if step == FAR - 1 else ref
        sems = (right_send, right_recv) if to_right else (left_send, left_recv)
        copy = remote(
            ref, target, sems[0].at[step, half], sems[1].at[step, half],
            p, right if to_right else left,
        )
        copy.start()
        sent.append(copy)
        flying[to_right, half] = copy

    across = []

    def cross(slot, source_z, half):
        start, size = CUT[half]
        held, at = (far, core) if slot == 2 * FAR - 1 else (shards, source_z * 2 + core)
        ref = held.at[at, pl.ds(start, size)]
        copy = remote(ref, ref, core_send.at[slot, half], core_recv.at[slot, half], p, sibling)
        copy.start()
        across.append(copy)

    def forward(step, half):
        for to_right in (True, False):
            if step == FAR and to_right != (half == 0):
                continue
            flying[to_right, half].wait_recv()
            source_z = (z - step + N_Z) % N_Z if to_right else (z + step) % N_Z
            if step < FAR - 1 or (step == FAR - 1 and to_right == (half == 0)):
                go(step, half, to_right)
            if step == FAR:
                slot = 2 * FAR - 1
            else:
                slot = 2 * step - 1 if to_right else 2 * step
            cross(slot, source_z, half)

    def begin(half, picks):
        for copy in picks:
            copy.wait_recv()
        go(0, half, True)
        go(0, half, False)
        cross(0, z, half)

    begin(0, picks_a)
    picks_b = pick(1, came_b, shards.at[e])
    queries(0, 2)
    begin(1, picks_b)
    came_low = spread_pieces(2)
    state_copies = []
    for k, t in enumerate(others):
        copy = remote(states.at[p], states.at[p], state_send.at[k], state_recv.at[k], t, e)
        copy.start()
        state_copies.append(copy)
    sent.extend(state_copies)
    forward(1, 0)
    queries(2, 5)
    picks_low = pick(2, came_low, low)
    forward(1, 1)
    queries(5, 8)
    forward(2, 0)
    part2[:DIM] = shards[e, :DIM]
    for copy in picks_low:
        copy.wait_recv()
    part2[DIM:] = low[:DIM]
    part_done = pltpu.make_async_copy(part2, part_out, local_sem.at[1])
    part_done.start()
    positives(0, 2)
    forward(2, 1)
    positives(2, 5)
    forward(3, 0)
    positives(5, 8)
    dst_acc[:DIM] = dst_acc[:DIM] + dst_acc[DIM:]
    forward(3, 1)

    def gather(j):
        hot = onehot(near_ids[j], ROWS)
        found = jnp.dot(shards[plan[j], :DIM], hot, preferred_element_type=F32)
        if j >= NEAR_BLOCKS:
            hot = onehot(far_ids[j - NEAR_BLOCKS], ROWS)
            found += jnp.dot(far[plan[QTOTAL + j]], hot, preferred_element_type=F32)
        negs[:, j * BLOCK : (j + 1) * BLOCK] = found.astype(BF16)
        negs_t[j * BLOCK : (j + 1) * BLOCK, :] = found.T.astype(BF16)

    def negatives(first, last, chunk_from=0, chunk_to=N_CHUNK):
        @pl.loop(chunk_from, chunk_to)
        def _(i):
            cols = chunk_cols(i)
            scores = jnp.dot(
                negs_t[first:last], query_b[:, cols], preferred_element_type=F32
            )
            coef = (0.5 * weight + 0.5 * weight * jnp.tanh(0.5 * scores)).astype(BF16)
            if first < EARLY:
                hold[:, cols] += jnp.dot(
                    negs[:, first:last], coef, preferred_element_type=F32
                )
            else:
                coefs[first - EARLY : last - EARLY, cols] = coef
            added = lax.dot_general(
                query_b[:, cols], coef, BY_COLS, preferred_element_type=F32
            )
            for j in range(first // BLOCK, last // BLOCK):
                at = j * BLOCK - first
                neg_grad[j] += added[:, at : at + BLOCK]

    for copy in across:
        copy.wait()
    across.clear()
    for j in range(NEAR_BLOCKS):
        gather(j)
    negatives(0, EARLY, 0, 4)
    forward(4, 0)
    forward(4, 1)
    negatives(0, EARLY, 4, 8)
    for copy in across:
        copy.wait()
    for j in range(NEAR_BLOCKS, QTOTAL):
        gather(j)

    for copy in sent:
        copy.wait_send()
    sent.clear()

    give_copies = {}

    def dense(g):
        first = plan[2 * QTOTAL + g]
        owner = ((z + DISTANCES[g // 2]) % N_Z) * 2 + (core if g % 2 == 0 else 1 - core)
        parts = jnp.concatenate([neg_grad[first + b] for b in range(QMAX)], axis=1)
        ids = jnp.concatenate([slots[owner * QMAX + b] for b in range(QMAX)], axis=1)
        hot = onehot(ids, ROWS)
        stacked = jnp.concatenate(split(parts), axis=0)
        summed = lax.dot_general(stacked, hot, BY_COLS, preferred_element_type=F32)
        return summed[:DIM] + summed[DIM:]

    def contribute(at):
        at = N_Z - 1 - at
        d = DISTANCES[at]
        shards[N_Z + d, :DIM] = dense(2 * at + 1).astype(BF16)
        copy = remote(
            shards.at[N_Z + d, pl.ds(0, DIM)], taken.at[d],
            give_send.at[d], give_recv.at[d], p, sibling,
        )
        copy.start()
        sent.append(copy)
        give_copies[d] = copy
        shards[d, :DIM] = dense(2 * at).astype(BF16)

    joined = set()
    ring = {}

    def reduce_step(step, half, ways=(True, False)):
        d = FAR - step
        start, size = CUT[half]
        rows = pl.ds(start, size)
        for to_right in ways:
            if step == 0 and to_right != (half == 0):
                continue
            place = d if to_right else (N_Z - d) % N_Z
            if place not in joined:
                give_copies[place].wait_recv()
                joined.add(place)
            value = shards[place, rows].astype(F32) + taken[place, rows].astype(F32)
            got = got_right if to_right else got_left
            if step >= 2 or (step == 1 and to_right == (half == 0)):
                ring[to_right, half].wait_recv()
                value = value + got[step - 1, rows].astype(F32)
            shards[place, rows] = value.astype(BF16)
            send, recv = (down_send, down_recv) if to_right else (up_send, up_recv)
            copy = remote(
                shards.at[place, rows], got.at[step, rows],
                send.at[step, half], recv.at[step, half], p, right if to_right else left,
            )
            copy.start()
            ring[to_right, half] = copy
            sent.append(copy)

    def query_grads(first, last):
        @pl.loop(first, last)
        def _(i):
            cols = chunk_cols(i)
            src_hot = onehot(src_ids[:, cols], ROWS)
            rel_hot, r_re, r_im = relation_rows(cols)
            s_re, s_im = source[:HALF, cols], source[HALF:, cols]
            g = jnp.dot(negs[:, EARLY:], coefs[:, cols], preferred_element_type=F32)
            g_re = hold[:HALF, cols] + g[:HALF]
            g_im = hold[HALF:, cols] + g[HALF:]
            put_split(spread, *back(g_re, g_im, r_re, r_im))
            src_acc[...] += lax.dot_general(
                spread[...], src_hot, BY_COLS, preferred_element_type=F32
            )
            put_split(spread, *back(g_re, g_im, s_re, s_im))
            rel_acc[...] += lax.dot_general(
                spread[...], rel_hot, BY_COLS, preferred_element_type=F32
            )

    negatives(1024, 1536)
    contribute(0)
    reduce_step(0, 0)
    reduce_step(0, 1)
    negatives(512, 1024)
    contribute(1)
    contribute(2)
    for way in (True, False):
        for half in range(2):
            reduce_step(1, half, (way,))
    contribute(3)
    contribute(4)
    query_grads(0, 3)
    reduce_step(2, 0)
    query_grads(3, 4)
    contribute(5)
    contribute(6)
    reduce_step(2, 1)
    query_grads(4, 7)
    contribute(7)
    reduce_step(3, 0)
    query_grads(7, 8)
    reduce_step(3, 1)

    rel_grad = (rel_acc[:DIM] + rel_acc[DIM:]).T
    for r in range(NREL):
        rel_mine[r] = rel_grad[r : r + 1]
    first_copies = []
    for k, t in enumerate(others):
        copy = remote(
            rel_mine.at[t], rel_rows.at[p], rel_send.at[0, k], rel_recv.at[0, k], t, e
        )
        copy.start()
        first_copies.append(copy)
    rel_rows[p] = rel_mine[p]

    new_state = src_state[...]
    grad = src_acc[:DIM] + src_acc[DIM:]
    src_step, src_state_out[...] = adagrad(new_state, grad)
    src_acc[:DIM] = src_step
    src_done = pltpu.make_async_copy(src_acc.at[pl.ds(0, DIM)], src_step_out, local_sem.at[2])
    src_done.start()

    for copy in first_copies:
        copy.wait_recv()
    rel_sums[e] = jnp.sum(rel_rows[...], axis=0)
    second_copies = []
    for k, t in enumerate(edge_others):
        copy = remote(
            rel_sums.at[e], rel_sums.at[e], rel_send.at[1, k], rel_recv.at[1, k], p, t
        )
        copy.start()
        second_copies.append(copy)

    for copy in state_copies:
        copy.wait_recv()
    part_state = states[matching[p]]
    give_copies[0].wait_recv()
    dst_acc[:DIM] = dst_acc[:DIM] + shards[0, :DIM].astype(F32) + taken[0].astype(F32)

    for copy in second_copies:
        copy.wait_recv()
    rel_out[p] = jnp.sum(rel_sums[...], axis=0)
    third_copies = []
    for k, t in enumerate(others):
        copy = remote(rel_out.at[p], rel_out.at[p], rel_send.at[2, k], rel_recv.at[2, k], t, e)
        copy.start()
        third_copies.append(copy)

    for half in range(2):
        ring[True, half].wait_recv()
        ring[False, half].wait_recv()
    grad = dst_acc[:DIM] + got_right[FAR - 1].astype(F32) + got_left[FAR - 1].astype(F32)
    dst_step, dst_state_out[...] = adagrad(part_state, grad)
    dst_acc[:DIM] = dst_step
    dst_done = pltpu.make_async_copy(dst_acc.at[pl.ds(0, DIM)], dst_step_out, local_sem.at[3])
    dst_done.start()

    for copy in third_copies:
        copy.wait_recv()
    for copy in sent + first_copies + second_copies + third_copies:
        copy.wait_send()
    part_done.wait()
    src_done.wait()
    dst_done.wait()


def adagrad(state, grad):
    new_state = state + jnp.sum(grad * grad, axis=0, keepdims=True) * (1.0 / DIM)
    return learn_rate * grad / jnp.sqrt(new_state), new_state


def run(*args):
    dma = pltpu.SemaphoreType.DMA
    vmem = pl.BlockSpec(memory_space=VMEM)
    smem = pl.BlockSpec(memory_space=SMEM)
    hbm = pl.BlockSpec(memory_space=HBM)
    return pl.pallas_call(
        kernel,
        out_shape=(
            jax.ShapeDtypeStruct((DIM, ROWS), F32),
            jax.ShapeDtypeStruct((1, ROWS), F32),
            jax.ShapeDtypeStruct((2 * DIM, ROWS), BF16),
            jax.ShapeDtypeStruct((DIM, ROWS), F32),
            jax.ShapeDtypeStruct((1, ROWS), F32),
            jax.ShapeDtypeStruct((NREL, 1, DIM), F32),
        ),
        in_specs=[smem, smem, vmem, vmem, hbm] + [vmem] * 8,
        out_specs=(hbm, vmem, hbm, hbm, vmem, vmem),
        scratch_shapes=[
            VMEM((N_EDGE, PAD_DIM, ROWS), BF16),
            VMEM((2, DIM, ROWS), BF16),
            VMEM((PAD_DIM, ROWS), BF16),
            VMEM((2, PAD_DIM, ROWS), BF16),
            *(VMEM((N_DOM, size, PIECE_COLS), BF16) for _, _, size in PAIRED),
            *(VMEM((N_DOM - 1, size, PIECE_COLS), BF16) for _, _, size in PAIRED),
            VMEM((N_DOM, 1, ROWS), F32),
            VMEM((DIM, EDGES), F32),
            VMEM((2 * DIM, ROWS), BF16),
            VMEM((2 * DIM, ROWS), BF16),
            VMEM((2 * DIM, NREL), BF16),
            VMEM((DIM, EDGES), BF16),
            VMEM((DIM, EDGES), F32),
            VMEM((NNEG - EARLY, EDGES), BF16),
            VMEM((DIM, NNEG), BF16),
            VMEM((NNEG, DIM), BF16),
            VMEM((QTOTAL + QMAX, DIM, BLOCK), F32),
            VMEM((2 * DIM, CHUNK), BF16),
            VMEM((2 * DIM, ROWS), F32),
            VMEM((2 * DIM, ROWS), F32),
            VMEM((2 * DIM, NREL), F32),
            VMEM((N_Z, DIM, ROWS), BF16),
            VMEM((FAR, DIM, ROWS), BF16),
            VMEM((FAR, DIM, ROWS), BF16),
            VMEM((NREL, 1, DIM), F32),
            VMEM((N_DOM, 1, DIM), F32),
            VMEM((N_EDGE, 1, DIM), F32),
            dma((3, N_DOM - 1)), dma((3, N_DOM - 1)),
            dma((3, N_DOM - 1)), dma((3, N_DOM - 1)),
            dma((N_DOM - 1,)), dma((N_DOM - 1,)),
            dma((FAR, 2)), dma((FAR, 2)), dma((FAR, 2)), dma((FAR, 2)),
            dma((N_Z, 2)), dma((N_Z, 2)),
            dma((N_Z,)), dma((N_Z,)),
            dma((FAR, 2)), dma((FAR, 2)), dma((FAR, 2)), dma((FAR, 2)),
            dma((3, N_DOM - 1)), dma((3, N_DOM - 1)),
            dma((4,)),
        ],
        compiler_params=pltpu.CompilerParams(
            collective_id=0, has_side_effects=True, vmem_limit_bytes=60 * 2**20
        ),
        name="bucket_step",
    )(*args)


def finish_kernel(
    src_table, src_step, src_state, part, dst_step, dst_state, relation, rel_total,
    src_out, src_state_out, dst_out, dst_state_out, relation_out,
):
    src_out[...] = src_table[...] - src_step[...]
    src_state_out[...] = src_state[...]
    dst_out[...] = part[:DIM].astype(F32) + part[DIM:].astype(F32) - dst_step[...]
    dst_state_out[...] = dst_state[...]
    for r in range(NREL):
        relation_out[r : r + 1] = relation[r : r + 1] - rel_rate * rel_total[r]


def finish(*args):
    vmem = pl.BlockSpec(memory_space=VMEM)
    return pl.pallas_call(
        finish_kernel,
        out_shape=(
            jax.ShapeDtypeStruct((DIM, ROWS), F32),
            jax.ShapeDtypeStruct((1, ROWS), F32),
            jax.ShapeDtypeStruct((DIM, ROWS), F32),
            jax.ShapeDtypeStruct((1, ROWS), F32),
            jax.ShapeDtypeStruct((NREL, DIM), F32),
        ),
        in_specs=[vmem] * 8,
        out_specs=(vmem,) * 5,
        compiler_params=pltpu.CompilerParams(vmem_limit_bytes=60 * 2**20),
        name="finish",
    )(*args)


def shards(
    src_table,
    src_state,
    dst_table,
    dst_state,
    relation,
    edge_src,
    edge_dst,
    edge_rel,
    matching,
    neg_rows,
    quotas,
):
    plan, slots, near_ids, far_ids = make_plan(quotas, neg_rows.reshape(N_EDGE, QMAX * BLOCK))
    src_step, src_state_out, part, dst_step, dst_state_out, rel_total = run(
        matching,
        plan,
        dst_table,
        dst_state.reshape(1, ROWS),
        src_table,
        src_state.reshape(1, ROWS),
        relation.T,
        edge_src.reshape(1, EDGES),
        edge_dst.reshape(1, EDGES),
        edge_rel.reshape(1, EDGES),
        slots,
        near_ids,
        far_ids,
    )
    src_out, src_state_out, dst_out, dst_state_out, relation_out = finish(
        src_table, src_step, src_state_out, part, dst_step, dst_state_out, relation.T, rel_total
    )
    return (
        src_out,
        src_state_out.reshape(ROWS),
        dst_out,
        dst_state_out.reshape(ROWS),
        relation_out.T,
    )


def solution(mesh):
    in_specs = (
        P(None, ("dom", "edge")),
        P(("dom", "edge")),
        P(None, ("dom", "edge")),
        P(("dom", "edge")),
        P(),
        P(("dom", "edge")),
        P(("dom", "edge")),
        P(("dom", "edge")),
        P(),
        P(("dom", "edge"), None, None),
        P(("dom", "edge"), None),
    )
    out_specs = (
        P(None, ("dom", "edge")),
        P(("dom", "edge")),
        P(None, ("dom", "edge")),
        P(("dom", "edge")),
        P(),
    )
    return jax.shard_map(shards, mesh=mesh, in_specs=in_specs, out_specs=out_specs, check_vma=False)
```
